32 devices in a mesh: ep: 16 (over z, y, x), os: 2 (over core).
Axes of the slice: x: 2, y: 2, z: 4, core: 2. Of those that a mesh axis runs over, the one named last changes fastest.
Arguments:
- tokens: bfloat16 [2048, 2048], P('ep', 'os'), may hold values from -6 to 6
- cotangent: bfloat16 [2048, 2048], P('ep', 'os'), may hold values from -6 to 6
- expert_ids: int32 [2048, 8], P('ep'), may hold values from 0 to 15, all different within a row; in each aligned block of 128 rows (0 to 127, 128 to 255, ...) at most 96 rows name the same one
- route_weight: float32 [2048, 8], P('ep'), may hold values from 0.1 to 1
- placement: int32 [16], replicated, may hold values from 0 to 15, each once
- swap_flags: int32 [2, 16], replicated, may hold values from 0 to 1, as said below
- params: bfloat16 [16, 3, 2048, 384], P('ep', None, 'os'), may hold values from -1 to 1
- first_moment: bfloat16 [16, 3, 2048, 384], P('ep', None, 'os'), may hold values from -6 to 6
- second_moment: bfloat16 [16, 3, 2048, 384], P('ep', None, 'os'), may hold values from 0.5 to 20
Outputs:
- mixed: bfloat16 [2048, 2048], P('ep', 'os')
- input_grad: bfloat16 [2048, 2048], P('ep', 'os')
- new_params: bfloat16 [16, 3, 2048, 384], P('ep', None, 'os')
- new_first: bfloat16 [16, 3, 2048, 384], P('ep', None, 'os')
- new_second: bfloat16 [16, 3, 2048, 384], P('ep', None, 'os')
The draws below stay inside these ranges and needn't reach their ends.
Inputs may be any that keep to these rules, and one draw needn't show every extreme that they name: `expert_ids`: each row names 8 different experts; in each aligned block of 128 rows (the rows of one index of ep) no expert is named by more than 96 rows, a bound that some block reaches. `placement`: A permutation of the 16 expert ids. swap_flags[r, i] = swap_flags[r, i XOR 2^b_r] with b_0 = log2(16) - 1 and b_1 = 0.
All inputs are finite; a program needn't handle non-finite values.
Results may differ from the reference program's by a relative error of at most 0.023.
Values may be sent and summed in bfloat16 or wider, within the bound.
No kernel may reach another device: no remote copies, remote signals or barrier semaphores. Data moves between devices by JAX's collectives and lax.ppermute only.
A program may use at most 128 MiB of HBM per device.

```python
import math
import jax
import jax.numpy as jnp
import numpy as np
from jax import lax

D = 2048
TOP = 8
HW = 384
TOK_DEV = 128
EXPERTS = 16
TOKENS = 2048
CAP = 96
N_EP = 16
N_OS = 2


def draw_swap_flags(key, part):
    index = jnp.arange(EXPERTS, dtype=jnp.int32)
    bits = [EXPERTS.bit_length() - 2, 0]
    rounds = []
    for rnd in range(2):
        coins = jax.random.randint(jax.random.fold_in(key, rnd + 11), (EXPERTS,), 0, 2, dtype=jnp.int32)
        lowend = EXPERTS - 1 - (1 << bits[rnd])
        coins = coins.at[0].set(1).at[lowend].set(1)
        lower = index - (index & 1 << bits[rnd])
        rounds.append(coins[lower])
    return jnp.stack(rounds).astype(jnp.int32)


def draw_params(key, part):
    shape = (EXPERTS, 3, D, HW)
    base = jnp.clip(jax.random.normal(key, shape, jnp.float32), -6.0, 6.0)
    factor = jnp.where(jnp.arange(3) < 2, D ** (-0.5), HW ** (-0.5)).astype(jnp.float32).reshape(1, 3, 1, 1)
    return (base * factor).astype(jnp.bfloat16)


def block_levels(stream_key, dims, cuts, smallest, high):
    def one(dim, shards_of):
        steps = jax.random.uniform(jax.random.fold_in(jax.random.fold_in(stream_key, 6), dim), (shards_of,), jnp.float32, smallest / len(cuts), high / len(cuts))
        return jnp.repeat(jnp.exp(steps), dims[dim] // shards_of).reshape((-1,) + (1,) * (len(dims) - dim - 1))

    level = one(*cuts[0])
    for cut in cuts[1:]:
        level = level * one(*cut)
    return level


def shared_out(rng, own, number, rows, count, top, limit, lean):
    order = jax.random.permutation(rng, count)
    crowded, common = portions_of(count, rows * top, limit, lean, True), portions_of(count, rows * top, limit, lean, False)
    places = jnp.arange(count)

    def named(tallies, rotation):
        used = int((tallies > 0).sum())
        fixed = max(1, used // 4)
        shifted = fixed + (places - fixed + rotation * (used - fixed)) % max(1, count - fixed)
        return jnp.zeros((count,), jnp.int32).at[order[jnp.where(places < fixed, places, shifted)]].set(jnp.asarray(tallies, jnp.int32))

    tallies = jnp.where(number % 4 == 0, named(crowded, number // 4), named(common, number - number // 4 - 1))
    mixed = jax.random.permutation(jax.random.fold_in(own, 3), count)
    donor, taker = mixed[0:count // 2 * 2:2], mixed[1:count // 2 * 2:2]
    slack = jnp.minimum(tallies[donor] - 1, limit - tallies[taker]) // 2
    slack = jnp.where((donor == order[0]) | (taker == order[0]) | (tallies[taker] == 0), 0, jnp.maximum(slack, 0))
    shifted = jax.random.randint(jax.random.fold_in(own, 4), (count // 2,), 0, 1 << 20) % (slack + 1)
    tallies = tallies.at[donor].add(-shifted).at[taker].add(shifted)
    items = jnp.searchsorted(jnp.cumsum(tallies), jnp.arange(rows * top), side="right").astype(jnp.int32)
    listing = items.reshape(top, rows).T
    listing = listing[jax.random.permutation(jax.random.fold_in(own, 1), rows)]
    rotation = jax.random.randint(jax.random.fold_in(own, 2), (rows, 1), 0, top)
    return jnp.take_along_axis(listing, (jnp.arange(top)[None, :] + rotation) % top, axis=1)


def portions_of(count, total, most, skew, full):
    loads = [(1 << 20) // math.isqrt(standing ** skew) + 1 for standing in range(1, count + 1)]
    largest = most if full else min(most, max(-(-total // count), total * loads[0] // sum(loads)))
    least = 1 if total - largest >= count - 1 else 0
    holding, spare = [largest] + [least] * (count - 1), total - largest - least * (count - 1)
    while spare > 0:
        candidates = [i for i in range(1, count) if holding[i] < largest] or [i for i in range(1, count) if holding[i] < most]
        whole, budget = sum([loads[i] for i in candidates]), spare
        for i in candidates:
            extra = min(most - holding[i], max(1, budget * loads[i] // whole), spare)
            holding[i] = holding[i] + extra
            spare = spare - extra
    return np.array(holding)


def centred(stream_key, extent, deviation, reach, split=(), kind=jnp.bfloat16):
    result = deviation * jax.random.normal(stream_key, extent, jnp.float32)
    if split:
        result = result * block_levels(stream_key, extent, split, -0.22, 0.18)
    return jnp.clip(result, -reach, reach).astype(kind)


def setup_inputs(seed: int = 0) -> dict:
    key_of = jax.random.split(jax.random.key(seed), 10)
    tokens = centred(key_of[0], (TOKENS, D), 1.0, 6.0, ((0, 16), (1, 2)))
    cotangent = centred(key_of[1], (TOKENS, D), 1.0, 6.0, ((0, 16), (1, 2)))
    expert_ids_keys = jax.random.split(jax.random.fold_in(key_of[2], 1), TOKENS // TOK_DEV)
    expert_ids_turns = jax.random.permutation(jax.random.fold_in(key_of[2], 3), TOKENS // TOK_DEV)
    expert_ids = jax.vmap(lambda own, number: shared_out(jax.random.fold_in(key_of[2], 2), own, number, TOK_DEV, EXPERTS, TOP, CAP, 2))(expert_ids_keys, expert_ids_turns).reshape((TOKENS, TOP))
    route_weight = jnp.clip(jnp.exp(math.log(1.0) - 2.3025851 * jax.random.uniform(key_of[3], (TOKENS, TOP), jnp.float32) ** block_levels(key_of[3], (TOKENS, TOP), ((0, 16),), -0.2, 0.2)), 0.1, 1.0)
    placement = jax.random.permutation(key_of[4], EXPERTS).astype(jnp.int32)
    swap_flags = draw_swap_flags(jax.random.fold_in(key_of[9], 71), 0)
    params = draw_params(jax.random.fold_in(key_of[9], 71), 0)
    first_moment = centred(key_of[7], (EXPERTS, 3, D, HW), 1.0, 6.0, ((0, 16), (2, 2)))
    second_moment = jnp.clip(jnp.exp(math.log(20.0) - 3.6888795 * jax.random.uniform(key_of[8], (EXPERTS, 3, D, HW), jnp.float32) ** block_levels(key_of[8], (EXPERTS, 3, D, HW), ((0, 16), (2, 2)), -0.2, 0.2)), 0.5, 20.0).astype(jnp.bfloat16)
    return dict(tokens=tokens, cotangent=cotangent, expert_ids=expert_ids, route_weight=route_weight, placement=placement, swap_flags=swap_flags, params=params, first_moment=first_moment, second_moment=second_moment)


beta_first = 0.9
beta_second = 0.999
learn_rate = 0.01
adam_eps = 1e-08
adam_count = 10.0

def adam_update(weight, first, second, grad):
    first_new = beta_first * first.astype(jnp.float32) + (1.0 - beta_first) * grad
    second_new = beta_second * second.astype(jnp.float32) + (1.0 - beta_second) * grad * grad
    first_hat = first_new / (1.0 - beta_first ** adam_count)
    second_hat = second_new / (1.0 - beta_second ** adam_count)
    weight_new = weight.astype(jnp.float32) - learn_rate * first_hat / (jnp.sqrt(second_hat) + adam_eps)
    return (weight_new.astype(jnp.bfloat16), first_new.astype(jnp.bfloat16), second_new.astype(jnp.bfloat16))

def partial_sum(parts):
    rounded = parts.astype(jnp.bfloat16)
    rounded = lax.optimization_barrier(rounded)
    return lax.optimization_barrier(jnp.sum(rounded.astype(jnp.float32), axis=0))

def expert_pass(x_rows, dy_rows, weight):
    shard = D // N_OS
    xs = x_rows.astype(jnp.float32).reshape(-1, N_OS, shard)
    dys = dy_rows.astype(jnp.float32).reshape(-1, N_OS, shard)
    wfull = weight.astype(jnp.float32)
    wparts = wfull.reshape(3, N_OS, shard, HW)
    both = partial_sum(jnp.einsum('ros,kosh->okrh', xs, wparts[:2]))
    gate = both[0]
    up = both[1]
    sigma = jax.nn.sigmoid(gate)
    active = gate * sigma
    hidden = (active * up).astype(jnp.bfloat16)
    hidden_f = hidden.astype(jnp.float32)
    rows_out = jnp.einsum('rh,dh->rd', hidden_f, wfull[2]).astype(jnp.bfloat16)
    back = partial_sum(jnp.einsum('ros,osh->orh', dys, wparts[2]))
    d_gate = (back * up * sigma * (1.0 + gate * (1.0 - sigma))).astype(jnp.bfloat16)
    d_up = (back * active).astype(jnp.bfloat16)
    deriv = jnp.stack((d_gate, d_up)).astype(jnp.float32)
    x_f = x_rows.astype(jnp.float32)
    grad_in = jnp.einsum('rd,krh->kdh', x_f, deriv)
    grad_out = jnp.einsum('rd,rh->dh', dy_rows.astype(jnp.float32), hidden_f)
    grad = jnp.concatenate((grad_in, grad_out[None]), axis=0)
    rows_grad = jnp.einsum('krh,kdh->rd', deriv, wfull[:2]).astype(jnp.bfloat16)
    return (rows_out, rows_grad, grad)

def reference(tokens, cotangent, expert_ids, route_weight, placement, swap_flags, params, first_moment, second_moment):
    index = jnp.arange(EXPERTS, dtype=jnp.int32)
    place = placement
    state = (params, first_moment, second_moment)
    bits = [EXPERTS.bit_length() - 2, 0]
    for rnd in range(2):
        partner = index ^ 1 << bits[rnd]
        chosen = swap_flags[rnd] == 1
        state = tuple((jnp.where(chosen[:, None, None, None], s[partner], s) for s in state))
        place = jnp.where(chosen, place[partner], place)
    held_params, held_first, held_second = state
    holder = jnp.zeros((EXPERTS,), jnp.int32).at[place].set(index)
    dest = holder[expert_ids].reshape(N_EP, TOK_DEV * TOP)
    onehot = (dest[:, :, None] == index[None, None, :]).astype(jnp.int32)
    before = jnp.cumsum(onehot, axis=1) - onehot
    slot = lax.optimization_barrier(jnp.sum(before * onehot, axis=2)).astype(jnp.int32)
    source = jnp.broadcast_to(jnp.arange(N_EP, dtype=jnp.int32)[:, None], dest.shape)
    flat_rows = jnp.arange(TOKENS * TOP, dtype=jnp.int32).reshape(N_EP, TOK_DEV * TOP)
    table = jnp.zeros((EXPERTS, N_EP, CAP), jnp.int32).at[dest, source, slot].set(flat_rows + 1)
    weights_flat = route_weight.reshape(-1)

    def one_expert(carry, inputs):
        mixed_acc, grad_acc = carry
        rows, weight, first, second = inputs
        rows = rows.reshape(-1)
        filled = rows > 0
        src = jnp.maximum(rows - 1, 0).astype(jnp.int32)
        owner = (src // TOP).astype(jnp.int32)
        x_rows = jnp.where(filled[:, None], tokens[owner], jnp.zeros((), jnp.bfloat16))
        dy_rows = jnp.where(filled[:, None], weights_flat[src][:, None] * cotangent[owner].astype(jnp.float32), jnp.float32(0.0)).astype(jnp.bfloat16)
        rows_out, rows_grad, grad = expert_pass(x_rows, dy_rows, weight)
        scale = jnp.where(filled, weights_flat[src], jnp.float32(0.0))
        mixed_acc = mixed_acc.at[owner].add(scale[:, None] * rows_out.astype(jnp.float32))
        grad_acc = grad_acc.at[owner].add(jnp.where(filled[:, None], rows_grad.astype(jnp.float32), jnp.float32(0.0)))
        return ((mixed_acc, grad_acc), adam_update(weight, first, second, grad))
    init = (jnp.zeros((TOKENS, D), jnp.float32), jnp.zeros((TOKENS, D), jnp.float32))
    (mixed_acc, grad_acc), updated = lax.scan(one_expert, init, (table, held_params, held_first, held_second))
    new_params, new_first, new_second = updated
    return (mixed_acc.astype(jnp.bfloat16), grad_acc.astype(jnp.bfloat16), new_params, new_first, new_second)
```

```python
import jax
import jax.numpy as jnp
from jax import lax
from jax.sharding import PartitionSpec as P

beta_first = 0.9
beta_second = 0.999
learn_rate = 0.01
adam_eps = 1e-08
adam_count = 10.0


def from_partner(value, bit):
    return lax.ppermute(value, "ep", [(i, i ^ bit) for i in range(lax.axis_size("ep"))])


def sum_over_cores(value):
    if lax.axis_size("os") != 2:
        return lax.psum(value, "os").astype(jnp.float32)
    moved = lax.ppermute(value, "os", [(0, 1), (1, 0)])
    return value.astype(jnp.float32) + moved.astype(jnp.float32)


def adam_update(weight, first, second, grad):
    first_new = beta_first * first.astype(jnp.float32) + (1.0 - beta_first) * grad
    second_new = beta_second * second.astype(jnp.float32) + (1.0 - beta_second) * grad * grad
    first_hat = first_new / (1.0 - beta_first**adam_count)
    second_hat = second_new / (1.0 - beta_second**adam_count)
    weight_new = weight.astype(jnp.float32) - learn_rate * first_hat / (
        jnp.sqrt(second_hat) + adam_eps
    )
    return (
        weight_new.astype(jnp.bfloat16),
        first_new.astype(jnp.bfloat16),
        second_new.astype(jnp.bfloat16),
    )


def high_bits(experts):
    return [1 << b for b in range(experts.bit_length() - 2, 1, -1)]


def block_order(experts):
    order = [0]
    for bit in high_bits(experts):
        order = order + [r ^ bit for r in order]
    return [r ^ low for low in range(4) for r in order]


def gather_rows(block):
    experts = lax.axis_size("ep")
    for bit in high_bits(experts):
        block = jnp.concatenate((block, from_partner(block, bit)), axis=0)
    half = block.shape[1] // 2
    one = from_partner(block, 1)
    two = from_partner(block, 2)
    three = jnp.concatenate(
        (from_partner(two[:, :half], 1), from_partner(one[:, half:], 2)), axis=1
    )
    return jnp.concatenate((block, one, two, three), axis=0)


def add_rounded(*parts):
    total = parts[0].astype(jnp.float32)
    for part in parts[1:]:
        total = total + part.astype(jnp.float32)
    return total.astype(jnp.bfloat16)


def scatter_rows(rows):
    experts = lax.axis_size("ep")
    size = rows.shape[0] // 4
    half = rows.shape[1] // 2
    own, one, two, three = (rows[k * size : (k + 1) * size] for k in range(4))
    two_left = add_rounded(two[:, :half], from_partner(three[:, :half], 1))
    one_right = add_rounded(one[:, half:], from_partner(three[:, half:], 2))
    left = add_rounded(own[:, :half], from_partner(one[:, :half], 1), from_partner(two_left, 2))
    right = add_rounded(own[:, half:], from_partner(one_right, 1), from_partner(two[:, half:], 2))
    block = jnp.concatenate((left, right), axis=1)
    for bit in reversed(high_bits(experts)):
        keep = block.shape[0] // 2
        block = add_rounded(block[:keep], from_partner(block[keep:], bit))
    return block


def migrate(parts, own_flags, bits):
    result = []
    for part in parts:
        for rnd, bit in enumerate(bits):
            moved = from_partner(part, bit)
            part = jnp.where(own_flags[rnd], moved, part)
        result.append(part)
    return result


def dot(a, b, dims):
    return lax.dot_general(a, b, ((dims[:1], dims[1:]), ((), ())), preferred_element_type=jnp.float32)


def on_device(
    tokens,
    cotangent,
    expert_ids,
    route_weight,
    placement,
    swap_flags,
    params,
    first_moment,
    second_moment,
):
    experts = lax.axis_size("ep")
    mine = lax.axis_index("ep")
    index = jnp.arange(experts, dtype=jnp.int32)
    bits = [experts // 2, 1]
    place = placement
    own_flags = []
    for rnd in range(len(bits)):
        place = jnp.where(swap_flags[rnd] == 1, place[index ^ bits[rnd]], place)
        own_flags.append(swap_flags[rnd, mine] == 1)
    dense = jnp.sum(
        jnp.where(
            expert_ids.T[None, :, :] == index[:, None, None], route_weight.T[None, :, :], 0.0
        ),
        axis=1,
    )
    dense = lax.all_gather(dense, "ep")
    scale = lax.dynamic_index_in_dim(dense, place[mine], axis=1, keepdims=False)
    scale = scale[mine ^ jnp.array(block_order(experts), jnp.int32)].reshape(-1, 1)

    weight = migrate([params[0, k] for k in range(3)], own_flags, bits)
    x_rows = gather_rows(tokens)
    dy_rows = (scale * gather_rows(cotangent).astype(jnp.float32)).astype(jnp.bfloat16)

    gate = sum_over_cores(dot(x_rows, weight[0], (1, 0)).astype(jnp.bfloat16))
    up = sum_over_cores(dot(x_rows, weight[1], (1, 0)).astype(jnp.bfloat16))
    sigma = jax.nn.sigmoid(gate)
    active = gate * sigma
    hidden = (active * up).astype(jnp.bfloat16)
    mixed = scatter_rows((scale * dot(hidden, weight[2], (1, 1))).astype(jnp.bfloat16))

    back = sum_over_cores(dot(dy_rows, weight[2], (1, 0)).astype(jnp.bfloat16))
    d_gate = (back * up * sigma * (1.0 + gate * (1.0 - sigma))).astype(jnp.bfloat16)
    d_up = (back * active).astype(jnp.bfloat16)
    rows_grad = dot(d_gate, weight[0], (1, 1)) + dot(d_up, weight[1], (1, 1))
    input_grad = scatter_rows(rows_grad.astype(jnp.bfloat16))
    grad = [
        dot(x_rows, d_gate, (0, 0)),
        dot(x_rows, d_up, (0, 0)),
        dot(dy_rows, hidden, (0, 0)),
    ]
    first = migrate([first_moment[0, k] for k in range(3)], own_flags, bits)
    second = migrate([second_moment[0, k] for k in range(3)], own_flags, bits)
    updated = [adam_update(*state) for state in zip(weight, first, second, grad)]
    new_params, new_first, new_second = (jnp.stack(part)[None] for part in zip(*updated))
    return (mixed, input_grad, new_params, new_first, new_second)


def solution(mesh):
    state = P("ep", None, "os", None)
    rows = P("ep", "os")
    return jax.shard_map(
        on_device,
        mesh=mesh,
        in_specs=(rows, rows, P("ep", None), P("ep", None), P(), P(), state, state, state),
        out_specs=(rows, rows, state, state, state),
        check_vma=False,
    )
```

```python
import jax
import jax.numpy as jnp
from jax import lax
from jax.sharding import PartitionSpec as P

beta_first = 0.9
beta_second = 0.999
learn_rate = 0.01
adam_eps = 1e-08
adam_count = 10.0


def both(first, second):
    return lax.optimization_barrier((first, second))


def permute(value, pairs):
    return lax.ppermute(value, "ep", pairs)


def from_partner(value, bit):
    return permute(value, [(i, i ^ bit) for i in range(lax.axis_size("ep"))])


def sum_over_cores(value):
    if lax.axis_size("os") != 2:
        return lax.psum(value, "os").astype(jnp.float32)
    moved = lax.ppermute(value, "os", [(0, 1), (1, 0)])
    return value.astype(jnp.float32) + moved.astype(jnp.float32)


def adam_update(weight, first, second, grad):
    first_new = beta_first * first.astype(jnp.float32) + (1.0 - beta_first) * grad
    second_new = beta_second * second.astype(jnp.float32) + (1.0 - beta_second) * grad * grad
    first_hat = first_new / (1.0 - beta_first**adam_count)
    second_hat = second_new / (1.0 - beta_second**adam_count)
    weight_new = weight.astype(jnp.float32) - learn_rate * first_hat / (
        jnp.sqrt(second_hat) + adam_eps
    )
    return (
        weight_new.astype(jnp.bfloat16),
        first_new.astype(jnp.bfloat16),
        second_new.astype(jnp.bfloat16),
    )


def high_bits(experts):
    return [1 << b for b in range(experts.bit_length() - 2, 1, -1)]


def add_rounded(*parts):
    total = parts[0].astype(jnp.float32)
    for part in parts[1:]:
        total = total + part.astype(jnp.float32)
    return total.astype(jnp.bfloat16)


def planes():
    return [[i, i + 1, i + 2, i + 3] for i in range(0, lax.axis_size("ep"), 4)]


class Migration:
    def __init__(self, flags, slots):
        mine = lax.axis_index("ep")
        self.slots = slots
        self.mate = mate = mine & 3
        near = lax.dynamic_slice_in_dim(flags, mine - mate, 4, axis=1)
        index = jnp.arange(4, dtype=jnp.int32)
        swaps, turns = near[0], near[1]
        rank = jnp.sum(jnp.where(index[None, :] < index[:, None], swaps[None, :], 0), axis=1)
        chosen = (rank[None, :] == index[:, None]) & (swaps[None, :] == 1)
        active = jnp.sum(jnp.where(chosen, index[None, :], 0), axis=1)
        source = index ^ turns
        at_source = source[:, None] == index[None, :]
        swapped = jnp.sum(jnp.where(at_source, swaps[None, :], 0), axis=1)
        place = jnp.sum(jnp.where(at_source, rank[None, :], 0), axis=1)
        self.going = [active[slot] for slot in range(slots)]
        self.stayed = [source[dest] for dest in range(4)]
        self.crossed = [place[dest] for dest in range(4)]
        self.swapped = [swapped[dest] for dest in range(4)]

    def scalars(self):
        return self.going, self.stayed, self.crossed, self.swapped


def spread(array):
    k, rows, width = array.shape
    quarters = array.reshape(k, 4, rows // 4, width).transpose(1, 0, 2, 3)
    return lax.all_to_all(quarters, "ep", 0, 0, tiled=True, axis_index_groups=planes())


def to_cross(going, pool):
    return jnp.concatenate([lax.dynamic_slice_in_dim(pool, e, 1, axis=0) for e in going])


def pick(facts, pool, came):
    quarters = []
    for stayed, crossed, swapped in zip(*facts):
        stayed = lax.dynamic_slice_in_dim(pool, stayed, 1, axis=0)
        crossed = lax.dynamic_slice_in_dim(came, crossed, 1, axis=0)
        quarters.append(jnp.where(swapped == 1, crossed, stayed))
    return jnp.concatenate(quarters)


def collect(quarters):
    quarters = lax.all_to_all(quarters, "ep", 0, 0, tiled=True, axis_index_groups=planes())
    quarters = quarters.transpose(1, 0, 2, 3)
    return quarters.reshape(quarters.shape[0], -1, quarters.shape[-1])


def scatter_plane(rows):
    size = rows.shape[0] // 4
    half = rows.shape[1] // 2
    own, one, two, three = (rows[k * size : (k + 1) * size] for k in range(4))
    left = jnp.concatenate((one[:, :half], three[:, :half]))
    right = jnp.concatenate((two[:, half:], three[:, half:]))
    left, right = from_partner(left, 1), from_partner(right, 2)
    two_left = add_rounded(two[:, :half], left[size:])
    one_right = add_rounded(one[:, half:], right[size:])
    left = add_rounded(own[:, :half], left[:size], from_partner(two_left, 2))
    right = add_rounded(own[:, half:], right[:size], from_partner(one_right, 1))
    return jnp.concatenate((left, right), axis=1)


def scatter_rest(block):
    for bit in reversed(high_bits(lax.axis_size("ep"))):
        keep = block.shape[0] // 2
        block = add_rounded(block[:keep], from_partner(block[keep:], bit))
    return block


def dot(a, b, dims):
    return lax.dot_general(a, b, ((dims[:1], dims[1:]), ((), ())), preferred_element_type=jnp.float32)


def body(
    slots,
    tokens,
    cotangent,
    expert_ids,
    route_weight,
    placement,
    swap_flags,
    params,
    first_moment,
    second_moment,
):
    experts = lax.axis_size("ep")
    mine = lax.axis_index("ep")
    index = jnp.arange(experts, dtype=jnp.int32)
    place = placement
    for rnd, bit in enumerate((experts // 2, 1)):
        place = jnp.where(swap_flags[rnd] == 1, place[index ^ bit], place)
    table = jnp.sum(
        jnp.where(
            expert_ids.T[None, :, :] == index[:, None, None], route_weight.T[None, :, :], 0.0
        ),
        axis=1,
    )
    tok_rows, shard = tokens.shape
    half = shard // 2
    far = experts // 2

    def group(part, *operands):
        if lax.axis_size("os") != 2:
            return part(*operands)
        shapes = jax.eval_shape(part, *operands)
        return lax.cond(
            swap_flags[0, 0] >= 0,
            part,
            lambda *_: jax.tree.map(lambda x: jnp.zeros(x.shape, x.dtype), shapes),
            *operands,
        )

    terms = []
    for _ in range(3):
        terms.append(lax.reduce_precision(table, 8, 7))
        table = table - terms[-1]
    terms = jnp.stack(terms).astype(jnp.bfloat16).reshape(-1, shard)
    used = terms.shape[0]
    terms = jnp.pad(terms, ((0, -used % 16), (0, 0)))
    block = jnp.concatenate((tokens, cotangent, terms))[None]

    bits = high_bits(experts)

    def over_z(block, params):
        for bit in bits:
            block = jnp.concatenate((block, from_partner(block, bit)))
        pool = spread(params)
        facts = Migration(swap_flags, slots).scalars()
        return block, pool, to_cross(facts[0], pool), facts

    block, w_pool, w_going, facts = group(over_z, block, params[0])
    going, facts = facts[0], facts[1:]
    w_came = from_partner(w_going, far)

    def to_neighbours(block, first_moment):
        one, two = from_partner(block, 1), from_partner(block, 2)
        pool = spread(first_moment)
        return one, two, one[..., half:], two[..., :half], pool, to_cross(going, pool)

    one, two, one_right, two_left, m_pool, m_going = group(to_neighbours, block, first_moment[0])
    w_came, m_going = both(w_came, m_going)
    m_came = from_partner(m_going, far)

    def to_diagonal(block, one, two, one_right, two_left, w_pool, w_came):
        three = jnp.concatenate((from_partner(two_left, 1), from_partner(one_right, 2)), axis=-1)
        weight = collect(pick(facts, w_pool, w_came))
        blocks = (block, one, two, three)
        x_rows = jnp.concatenate([b[:, :tok_rows] for b in blocks]).reshape(-1, shard)
        dy_rows = jnp.concatenate([b[:, tok_rows : 2 * tok_rows] for b in blocks]).reshape(-1, shard)
        terms = jnp.concatenate([b[:, 2 * tok_rows : 2 * tok_rows + used] for b in blocks])
        terms = terms.reshape(-1, 3, experts, tok_rows)
        terms = lax.dynamic_index_in_dim(terms, place[mine], axis=2, keepdims=False)
        scale = jnp.sum(terms.astype(jnp.float32), axis=1).reshape(-1, 1)
        dy_rows = (scale * dy_rows.astype(jnp.float32)).astype(jnp.bfloat16)
        return weight, x_rows, dy_rows, scale

    weight, x_rows, dy_rows, scale = group(
        to_diagonal, block, one, two, one_right, two_left, w_pool, w_came
    )

    def expert(weight, x_rows, dy_rows, scale, second_moment):
        pool = spread(second_moment)
        down = weight[2]
        gate_up = jnp.concatenate((weight[0], weight[1]), axis=1)
        width = down.shape[-1]
        gate_up_out = sum_over_cores(dot(x_rows, gate_up, (1, 0)).astype(jnp.bfloat16))
        back = sum_over_cores(dot(dy_rows, down, (1, 0)).astype(jnp.bfloat16))
        gate, up = gate_up_out[:, :width], gate_up_out[:, width:]
        sigma = jax.nn.sigmoid(gate)
        active = gate * sigma
        hidden = (active * up).astype(jnp.bfloat16)
        mixed_rows = (scale * dot(hidden, down, (1, 1))).astype(jnp.bfloat16)
        d_gate = (back * up * sigma * (1.0 + gate * (1.0 - sigma))).astype(jnp.bfloat16)
        d_up = (back * active).astype(jnp.bfloat16)
        deriv = jnp.concatenate((d_gate, d_up), axis=1)
        grad_rows = dot(deriv, gate_up, (1, 1)).astype(jnp.bfloat16)
        grad_rows, pool = both(grad_rows, pool)
        return mixed_rows, grad_rows, hidden, deriv, pool, to_cross(going, pool)

    mixed_rows, grad_rows, hidden, deriv, v_pool, v_going = group(
        expert, weight, x_rows, dy_rows, scale, second_moment[0]
    )
    v_came = from_partner(v_going, far)

    def to_owners(mixed_rows, grad_rows, x_rows, dy_rows, hidden, deriv, m_pool, m_came):
        width = hidden.shape[-1]
        mixed = scatter_plane(mixed_rows)
        input_grad = scatter_plane(grad_rows)
        first = collect(pick(facts, m_pool, m_came))
        grad_in = dot(x_rows, deriv, (0, 0))
        grad = (grad_in[:, :width], grad_in[:, width:], dot(dy_rows, hidden, (0, 0)))
        return mixed, input_grad, first, grad

    mixed, input_grad, first, grad = group(
        to_owners, mixed_rows, grad_rows, x_rows, dy_rows, hidden, deriv, m_pool, m_came
    )
    second = collect(pick(facts, v_pool, v_came))
    mixed, input_grad = scatter_rest(mixed), scatter_rest(input_grad)
    updated = [adam_update(weight[k], first[k], second[k], grad[k]) for k in range(3)]
    return (mixed, input_grad, *(jnp.stack(part)[None] for part in zip(*updated)))


def on_device(*args):
    swap_flags = args[5]
    if lax.axis_size("os") != 2:
        return body(4, *args)
    most = jnp.max(jnp.sum(swap_flags[0].reshape(-1, 4), axis=1))
    return lax.cond(
        most <= 3, lambda *a: body(3, *a), lambda *a: body(4, *a), *args
    )


def solution(mesh):
    state = P("ep", None, "os", None)
    rows = P("ep", "os")
    return jax.shard_map(
        on_device,
        mesh=mesh,
        in_specs=(rows, rows, P("ep", None), P("ep", None), P(), P(), state, state, state),
        out_specs=(rows, rows, state, state, state),
        check_vma=False,
    )
```

```python
import functools

import jax
import jax.numpy as jnp
from jax import lax
from jax.experimental import pallas as pl
from jax.experimental.pallas import tpu as pltpu
from jax.sharding import PartitionSpec as P

beta_first = 0.9
beta_second = 0.999
learn_rate = 0.01
adam_eps = 1e-08
adam_count = 10.0


def both(first, second):
    return lax.optimization_barrier((first, second))


def permute(value, pairs):
    return lax.ppermute(value, "ep", pairs)


def from_partner(value, bit):
    return permute(value, [(i, i ^ bit) for i in range(lax.axis_size("ep"))])


def over_cores(value):
    if lax.axis_size("os") != 2:
        return (lax.psum(value, "os"),)
    return value, lax.ppermute(value, "os", [(0, 1), (1, 0)])


def adam_kernel(weight, moments, grad_gate, grad_up, grad_down, new_weight, new_first, new_second):
    for k, grad_ref in enumerate((grad_gate, grad_up, grad_down)):
        grad = grad_ref[...]
        first = beta_first * moments[0, k].astype(jnp.float32) + (1.0 - beta_first) * grad
        second = (
            beta_second * moments[0, 3 + k].astype(jnp.float32) + (1.0 - beta_second) * grad * grad
        )
        first_hat = first / (1.0 - beta_first**adam_count)
        second_hat = second / (1.0 - beta_second**adam_count)
        new_weight[0, k] = (
            weight[k].astype(jnp.float32) - learn_rate * first_hat / (jnp.sqrt(second_hat) + adam_eps)
        ).astype(jnp.bfloat16)
        new_first[0, k] = first.astype(jnp.bfloat16)
        new_second[0, k] = second.astype(jnp.bfloat16)


def adam_update(weight, moments, grad):
    _, rows, width = weight.shape
    parts = 8 if rows % 128 == 0 else 4
    size = rows // parts
    per_quarter = parts // 4
    state = jax.ShapeDtypeStruct((1, 3, rows, width), jnp.bfloat16)
    return pl.pallas_call(
        adam_kernel,
        out_shape=(state,) * 3,
        grid=(parts,),
        in_specs=[
            pl.BlockSpec((3, size, width), lambda i: (0, i, 0)),
            pl.BlockSpec(
                (1, 6, size, width), lambda i: (i // per_quarter, 0, i % per_quarter, 0)
            ),
        ]
        + [pl.BlockSpec((size, width), lambda i: (i, 0))] * 3,
        out_specs=(pl.BlockSpec((1, 3, size, width), lambda i: (0, 0, i, 0)),) * 3,
        compiler_params=pltpu.CompilerParams(vmem_limit_bytes=32 * 1024 * 1024),
        cost_estimate=pl.CostEstimate(
            flops=40 * weight.size, transcendentals=2 * weight.size, bytes_accessed=16 * weight.size
        ),
    )(weight, moments, *grad)


def high_bits(experts):
    return [1 << b for b in range(experts.bit_length() - 2, 1, -1)]


def add_rounded(*parts):
    total = parts[0].astype(jnp.float32)
    for part in parts[1:]:
        total = total + part.astype(jnp.float32)
    return total.astype(jnp.bfloat16)


def planes():
    return [[i, i + 1, i + 2, i + 3] for i in range(0, lax.axis_size("ep"), 4)]


class Migration:
    def __init__(self, flags):
        mine = lax.axis_index("ep")
        self.mate = mate = mine & 3
        near = lax.dynamic_slice_in_dim(flags, mine - mate, 4, axis=1)
        index = jnp.arange(4, dtype=jnp.int32)
        swaps, turns = near[0], near[1]
        rank = jnp.sum(jnp.where(index[None, :] < index[:, None], swaps[None, :], 0), axis=1)
        chosen = (rank[None, :] == index[:, None]) & (swaps[None, :] == 1)
        active = jnp.sum(jnp.where(chosen, index[None, :], 0), axis=1)
        source = index ^ turns
        at_source = source[:, None] == index[None, :]
        swapped = jnp.sum(jnp.where(at_source, swaps[None, :], 0), axis=1)
        place = jnp.sum(jnp.where(at_source, rank[None, :], 0), axis=1)
        self.facts = jnp.concatenate((active, source, place, swapped))


def spread(array):
    k, rows, width = array.shape
    quarters = array.reshape(k, 4, rows // 4, width).transpose(1, 0, 2, 3)
    return lax.all_to_all(quarters, "ep", 0, 0, tiled=True, axis_index_groups=planes())


def to_cross(facts, slots, *pools, ahead=0):
    k = pools[0].shape[1]
    rest = pools[0].shape[2:]

    def kernel(facts, *refs):
        for i in range(len(pools)):
            refs[-1][:, i * k : (i + 1) * k] = refs[i][...]

    block = (1, k) + rest
    width = len(pools) * k
    return pl.pallas_call(
        kernel,
        out_shape=jax.ShapeDtypeStruct((slots, width) + rest, pools[0].dtype),
        grid_spec=pltpu.PrefetchScalarGridSpec(
            num_scalar_prefetch=1,
            grid=(slots,),
            in_specs=[pl.BlockSpec(block, lambda i, facts: (facts[ahead + i], 0, 0, 0))] * len(pools),
            out_specs=pl.BlockSpec((1, width) + rest, lambda i, facts: (i, 0, 0, 0)),
        ),
        compiler_params=pltpu.CompilerParams(vmem_limit_bytes=32 * 1024 * 1024),
        cost_estimate=pl.CostEstimate(
            flops=0, transcendentals=0, bytes_accessed=4 * slots * width * pools[0][0, 0].size
        ),
    )(facts, *pools)


def pick(facts, pool, came, *picked):
    slots, k = came.shape[:2]
    rest = came.shape[2:]
    ahead = len(picked) * k

    def kernel(facts, pool, came, *refs):
        out = refs[-1]
        swapped = facts[12 + pl.program_id(0)] == 1

        @pl.when(swapped)
        def _():
            out[:, ahead:] = came[...]

        @pl.when(jnp.logical_not(swapped))
        def _():
            out[:, ahead:] = pool[...]

        for i in range(len(picked)):
            out[:, i * k : (i + 1) * k] = refs[i][...]

    block = (1, k) + rest
    width = ahead + k
    return pl.pallas_call(
        kernel,
        out_shape=jax.ShapeDtypeStruct((4, width) + rest, came.dtype),
        grid_spec=pltpu.PrefetchScalarGridSpec(
            num_scalar_prefetch=1,
            grid=(4,),
            in_specs=[
                pl.BlockSpec(block, lambda i, facts: (facts[4 + i], 0, 0, 0)),
                pl.BlockSpec(block, lambda i, facts: (jnp.minimum(facts[8 + i], slots - 1), 0, 0, 0)),
            ]
            + [pl.BlockSpec(block, lambda i, facts: (i, 0, 0, 0))] * len(picked),
            out_specs=pl.BlockSpec((1, width) + rest, lambda i, facts: (i, 0, 0, 0)),
        ),
        compiler_params=pltpu.CompilerParams(vmem_limit_bytes=32 * 1024 * 1024),
        cost_estimate=pl.CostEstimate(
            flops=0, transcendentals=0, bytes_accessed=2 * (2 * width + k) * pool[:, 0].size
        ),
    )(facts, pool, came, *picked)


def assemble_rows(tok_rows, blocks):
    n, rows, shard = blocks[0].shape
    parts = ((0, tok_rows), (tok_rows, tok_rows), (2 * tok_rows, rows - 2 * tok_rows))

    def kernel(*refs):
        sources, outs, sems = refs[: len(blocks)], refs[len(blocks) : -1], refs[-1]
        copies = [
            pltpu.make_async_copy(
                source.at[:, pl.ds(start, size)], out.at[pl.ds(i * n, n)], sems.at[i, p]
            )
            for i, source in enumerate(sources)
            for p, ((start, size), out) in enumerate(zip(parts, outs))
        ]
        for copy in copies:
            copy.start()
        for copy in copies:
            copy.wait()

    return pl.pallas_call(
        kernel,
        out_shape=tuple(
            jax.ShapeDtypeStruct((len(blocks) * n, size, shard), blocks[0].dtype) for _, size in parts
        ),
        in_specs=[pl.BlockSpec(memory_space=pl.ANY)] * len(blocks),
        out_specs=(pl.BlockSpec(memory_space=pltpu.VMEM),) * 3,
        scratch_shapes=[pltpu.SemaphoreType.DMA((len(blocks), 3))],
        compiler_params=pltpu.CompilerParams(vmem_limit_bytes=32 * 1024 * 1024),
        cost_estimate=pl.CostEstimate(
            flops=0, transcendentals=0, bytes_accessed=4 * len(blocks) * blocks[0].size
        ),
    )(*blocks)


def partial_kernel(x_rows, dy_rows, weight, out):
    for k, rows in enumerate((x_rows, x_rows, dy_rows)):
        out[k] = jnp.dot(rows[...], weight[k], preferred_element_type=jnp.float32).astype(
            jnp.bfloat16
        )


def partial_products(x_rows, dy_rows, weight):
    rows, shard = x_rows.shape
    width = weight.shape[-1]
    size = 256
    return pl.pallas_call(
        partial_kernel,
        out_shape=jax.ShapeDtypeStruct((3, rows, width), jnp.bfloat16),
        grid=(rows // size,),
        in_specs=[
            pl.BlockSpec((size, shard), lambda i: (i, 0)),
            pl.BlockSpec((size, shard), lambda i: (i, 0)),
            pl.BlockSpec((3, shard, width), lambda i: (0, 0, 0)),
        ],
        out_specs=pl.BlockSpec((3, size, width), lambda i: (0, i, 0)),
        compiler_params=pltpu.CompilerParams(vmem_limit_bytes=32 * 1024 * 1024),
        cost_estimate=pl.CostEstimate(
            flops=6 * rows * shard * width,
            transcendentals=0,
            bytes_accessed=2 * (2 * rows * shard + 3 * shard * width + 3 * rows * width),
        ),
    )(x_rows, dy_rows, weight)


def middle_kernel(*refs):
    *addends, scale, down, hidden_ref, d_gate_ref, d_up_ref, left, right = refs

    def total(k):
        value = addends[0][k].astype(jnp.float32)
        for addend in addends[1:]:
            value = value + addend[k].astype(jnp.float32)
        return value

    gate, up, back = total(0), total(1), total(2)
    sigma = jax.nn.sigmoid(gate)
    active = gate * sigma
    hidden = (active * up).astype(jnp.bfloat16)
    hidden_ref[...] = hidden
    d_gate_ref[...] = (back * up * sigma * (1.0 + gate * (1.0 - sigma))).astype(jnp.bfloat16)
    d_up_ref[...] = (back * active).astype(jnp.bfloat16)
    half = left.shape[1]
    for part, out in enumerate((left, right)):
        rows_out = lax.dot_general(
            hidden,
            down[0, part * half : (part + 1) * half],
            (((1,), (1,)), ((), ())),
            preferred_element_type=jnp.float32,
        )
        out[...] = (scale[...] * rows_out).astype(jnp.bfloat16)


def middle(addends, scale, weight):
    _, rows, width = addends[0].shape
    shard = weight.shape[1]
    size = 256
    narrow = jax.ShapeDtypeStruct((rows, width), jnp.bfloat16)
    wide = jax.ShapeDtypeStruct((rows, shard // 2), jnp.bfloat16)
    return pl.pallas_call(
        middle_kernel,
        out_shape=(narrow,) * 3 + (wide,) * 2,
        grid=(rows // size,),
        in_specs=[pl.BlockSpec((3, size, width), lambda i: (0, i, 0))] * len(addends)
        + [
            pl.BlockSpec((size, 1), lambda i: (i, 0)),
            pl.BlockSpec((1, shard, width), lambda i: (2, 0, 0)),
        ],
        out_specs=(pl.BlockSpec((size, width), lambda i: (i, 0)),) * 3
        + (pl.BlockSpec((size, shard // 2), lambda i: (i, 0)),) * 2,
        compiler_params=pltpu.CompilerParams(vmem_limit_bytes=32 * 1024 * 1024),
        cost_estimate=pl.CostEstimate(
            flops=2 * rows * shard * width,
            transcendentals=rows * width,
            bytes_accessed=2 * (9 * rows * width + rows * shard + shard * width),
        ),
    )(*addends, scale, weight)


def collect(quarters):
    quarters = lax.all_to_all(quarters, "ep", 0, 0, tiled=True, axis_index_groups=planes())
    quarters = quarters.transpose(1, 0, 2, 3)
    return quarters.reshape(quarters.shape[0], -1, quarters.shape[-1])


def scatter_plane(left, right):
    size, half = left.shape[0] // 4, left.shape[1]
    left_in = from_partner(left[size : 3 * size], 1)
    right_in = from_partner(right[2 * size :], 2)
    left_last = from_partner(add_rounded(left[3 * size :], left_in[size:]), 2)
    right_last = from_partner(add_rounded(right[size : 2 * size], right_in[:size]), 1)
    left = add_rounded(left[:size], left_in[:size], left_last)
    right = add_rounded(right[:size], right_in[size:], right_last)
    return jnp.concatenate((left, right), axis=1)


def scatter_rest(block):
    for bit in reversed(high_bits(lax.axis_size("ep"))):
        keep = block.shape[0] // 2
        block = add_rounded(block[:keep], from_partner(block[keep:], bit))
    return block


def dot(a, b, dims):
    return lax.dot_general(a, b, ((dims[:1], dims[1:]), ((), ())), preferred_element_type=jnp.float32)


def on_device(
    tokens,
    cotangent,
    expert_ids,
    route_weight,
    placement,
    swap_flags,
    params,
    first_moment,
    second_moment,
):
    experts = lax.axis_size("ep")
    mine = lax.axis_index("ep")
    index = jnp.arange(experts, dtype=jnp.int32)
    table = jnp.sum(
        jnp.where(
            expert_ids.T[None, :, :] == index[:, None, None], route_weight.T[None, :, :], 0.0
        ),
        axis=1,
    )
    tok_rows, shard = tokens.shape
    half = shard // 2
    far = experts // 2

    most = jnp.max(jnp.sum(swap_flags[0].reshape(-1, 4), axis=1))

    def group(part, *operands):
        if lax.axis_size("os") != 2:
            return part(*operands)
        shapes = jax.eval_shape(part, *operands)
        return lax.cond(
            most >= 0,
            part,
            lambda *_: jax.tree.map(lambda x: jnp.zeros(x.shape, x.dtype), shapes),
            *operands,
        )

    terms = []
    for _ in range(3):
        terms.append(lax.reduce_precision(table, 8, 7))
        table = table - terms[-1]
    terms = jnp.stack(terms).astype(jnp.bfloat16).reshape(-1, shard)
    used = terms.shape[0]
    terms = jnp.pad(terms, ((0, -used % 16), (0, 0)))
    block = jnp.concatenate((tokens, cotangent, terms))[None]

    bits = high_bits(experts)

    def over_z(block, params):
        parts = [block]
        for bit in bits[:-1]:
            parts = parts + [from_partner(part, bit) for part in parts]
        other = jnp.concatenate([from_partner(part, bits[-1]) for part in parts])
        block = jnp.concatenate(parts)
        one, two = from_partner(block, 1), from_partner(block, 2)
        pool = spread(params)
        facts = Migration(swap_flags).facts
        place = placement
        for rnd, bit in enumerate((experts // 2, 1)):
            place = jnp.where(swap_flags[rnd] == 1, place[index ^ bit], place)
        facts = jnp.concatenate((facts, place[mine][None]))
        going = (to_cross(facts, 3, pool), to_cross(facts, 1, pool, ahead=3))
        return block, other, one, two, pool, going, facts

    block, other, one, two, w_pool, w_going, facts = group(over_z, block, params[0])

    def rest(slots, block, other, one, two, w_pool, w_going, facts, first_moment, second_moment):
        return after_z(
            slots, group, tok_rows, used, block, other, one, two, w_pool, w_going, facts,
            first_moment, second_moment,
        )

    operands = (
        block, other, one, two, w_pool, w_going, facts, first_moment[0], second_moment[0],
    )
    if lax.axis_size("os") != 2:
        return rest(4, *operands)
    return lax.cond(
        most <= 3, functools.partial(rest, 3), functools.partial(rest, 4), *operands
    )


def after_z(
    slots, group, tok_rows, used, block, other, one, two, w_pool, w_going, facts,
    first_moment, second_moment,
):
    experts = lax.axis_size("ep")
    far = experts // 2
    shard = block.shape[-1]
    half = shard // 2
    w_came = from_partner(w_going[0] if slots == 3 else jnp.concatenate(w_going), far)

    def to_neighbours(other, one, two, first_moment):
        three = from_partner(two, 1)
        other_one, other_two = from_partner(other, 1), from_partner(other, 2)
        other_three = from_partner(other_one, 2)
        pool = spread(first_moment)
        return three, other_one, other_two, other_three, pool, to_cross(facts, slots, pool)

    three, other_one, other_two, other_three, m_pool, m_going = group(
        to_neighbours, other, one, two, first_moment
    )
    w_came, m_going = both(w_came, m_going)
    m_came = from_partner(m_going, far)

    def assemble(w_pool, w_came, *blocks):
        x_rows, dy_rows, terms = assemble_rows(tok_rows, blocks)
        weight = collect(pick(facts, w_pool, w_came))
        terms = terms[:, :used].reshape(-1, 3, experts, tok_rows)
        terms = lax.dynamic_index_in_dim(terms, facts[16], axis=2, keepdims=False)
        scale = jnp.sum(terms.astype(jnp.float32), axis=1).reshape(-1, 1)
        dy_rows = dy_rows.reshape(-1, shard).astype(jnp.float32)
        dy_rows = (scale * dy_rows).astype(jnp.bfloat16)
        return weight, x_rows.reshape(-1, shard), dy_rows, scale

    weight, x_rows, dy_rows, scale = group(
        assemble, w_pool, w_came, block, other, one, other_one, three, other_three, two, other_two
    )
    def forward(weight, x_rows, dy_rows, scale, second_moment):
        pool = spread(second_moment)
        addends = group(over_cores, partial_products(x_rows, dy_rows, weight))
        hidden, d_gate, d_up, *mixed_rows = middle(addends, scale, weight)
        return hidden, d_gate, d_up, mixed_rows, pool

    hidden, d_gate, d_up, mixed_rows, v_pool = group(
        forward, weight, x_rows, dy_rows, scale, second_moment
    )
    v_came = from_partner(group(lambda pool: to_cross(facts, slots, pool), v_pool), far)

    def backward(weight, x_rows, dy_rows, hidden, d_gate, d_up, mixed_rows, m_pool, m_came):
        mixed = scatter_plane(*mixed_rows)
        grad_rows = [
            (dot(d_gate, weight[0, part], (1, 1)) + dot(d_up, weight[1, part], (1, 1))).astype(
                jnp.bfloat16
            )
            for part in (slice(0, half), slice(half, shard))
        ]
        input_grad = scatter_plane(*grad_rows)
        grad = (
            dot(x_rows, d_gate, (0, 0)),
            dot(x_rows, d_up, (0, 0)),
            dot(dy_rows, hidden, (0, 0)),
        )
        return mixed, input_grad, grad, pick(facts, m_pool, m_came)

    mixed, input_grad, grad, m_picked = group(
        backward, weight, x_rows, dy_rows, hidden, d_gate, d_up, mixed_rows, m_pool, m_came
    )

    def to_owners(mixed, input_grad, m_picked, v_pool, v_came):
        moments = lax.all_to_all(
            pick(facts, v_pool, v_came, m_picked),
            "ep",
            0,
            0,
            tiled=True,
            axis_index_groups=planes(),
        )
        return scatter_rest(mixed), scatter_rest(input_grad), moments

    mixed, input_grad, moments = group(
        to_owners, mixed, input_grad, m_picked, v_pool, v_came
    )
    return (mixed, input_grad, *adam_update(weight, moments, grad))


def solution(mesh):
    state = P("ep", None, "os", None)
    rows = P("ep", "os")
    return jax.shard_map(
        on_device,
        mesh=mesh,
        in_specs=(rows, rows, P("ep", None), P("ep", None), P(), P(), state, state, state),
        out_specs=(rows, rows, state, state, state),
        check_vma=False,
    )
```

```python
import functools

import jax
import jax.numpy as jnp
from jax import lax
from jax.experimental import pallas as pl
from jax.experimental.pallas import tpu as pltpu
from jax.sharding import PartitionSpec as P

beta_first = 0.9
beta_second = 0.999
learn_rate = 0.01
adam_eps = 1e-08
adam_count = 10.0


def both(first, second):
    return lax.optimization_barrier((first, second))


def permute(value, pairs):
    return lax.ppermute(value, "ep", pairs)


def from_partner(value, bit):
    return permute(value, [(i, i ^ bit) for i in range(lax.axis_size("ep"))])


def over_cores(value):
    if lax.axis_size("os") != 2:
        return (lax.psum(value, "os"),)
    return value, lax.ppermute(value, "os", [(0, 1), (1, 0)])


def adam_kernel(weight, moments, grad_gate, grad_up, grad_down, new_weight, new_first, new_second):
    for k, grad_ref in enumerate((grad_gate, grad_up, grad_down)):
        grad = grad_ref[...]
        first = beta_first * moments[0, k].astype(jnp.float32) + (1.0 - beta_first) * grad
        second = (
            beta_second * moments[0, 3 + k].astype(jnp.float32) + (1.0 - beta_second) * grad * grad
        )
        step = (learn_rate / (1.0 - beta_first**adam_count)) * first
        size = jnp.sqrt((1.0 / (1.0 - beta_second**adam_count)) * second) + adam_eps
        new_weight[0, k] = (weight[k].astype(jnp.float32) - step / size).astype(jnp.bfloat16)
        new_first[0, k] = first.astype(jnp.bfloat16)
        new_second[0, k] = second.astype(jnp.bfloat16)


def adam_update(weight, moments, grad):
    _, rows, width = weight.shape
    parts = 8 if rows % 128 == 0 else 4
    size = rows // parts
    per_quarter = parts // 4
    state = jax.ShapeDtypeStruct((1, 3, rows, width), jnp.bfloat16)
    return pl.pallas_call(
        adam_kernel,
        out_shape=(state,) * 3,
        grid=(parts,),
        in_specs=[
            pl.BlockSpec((3, size, width), lambda i: (0, i, 0)),
            pl.BlockSpec(
                (1, 6, size, width), lambda i: (i // per_quarter, 0, i % per_quarter, 0)
            ),
        ]
        + [pl.BlockSpec((size, width), lambda i: (i, 0))] * 3,
        out_specs=(pl.BlockSpec((1, 3, size, width), lambda i: (0, 0, i, 0)),) * 3,
        compiler_params=pltpu.CompilerParams(vmem_limit_bytes=32 * 1024 * 1024),
        cost_estimate=pl.CostEstimate(
            flops=40 * weight.size, transcendentals=2 * weight.size, bytes_accessed=16 * weight.size
        ),
    )(weight, moments, *grad)


def high_bits(experts):
    return [1 << b for b in range(experts.bit_length() - 2, 1, -1)]


def add_rounded(*parts):
    total = parts[0].astype(jnp.float32)
    for part in parts[1:]:
        total = total + part.astype(jnp.float32)
    return total.astype(jnp.bfloat16)


def planes():
    return [[i, i + 1, i + 2, i + 3] for i in range(0, lax.axis_size("ep"), 4)]


class Migration:
    def __init__(self, flags):
        mine = lax.axis_index("ep")
        self.mate = mate = mine & 3
        near = lax.dynamic_slice_in_dim(flags, mine - mate, 4, axis=1)
        index = jnp.arange(4, dtype=jnp.int32)
        swaps, turns = near[0], near[1]
        rank = jnp.sum(jnp.where(index[None, :] < index[:, None], swaps[None, :], 0), axis=1)
        chosen = (rank[None, :] == index[:, None]) & (swaps[None, :] == 1)
        active = jnp.sum(jnp.where(chosen, index[None, :], 0), axis=1)
        source = index ^ turns
        at_source = source[:, None] == index[None, :]
        swapped = jnp.sum(jnp.where(at_source, swaps[None, :], 0), axis=1)
        place = jnp.sum(jnp.where(at_source, rank[None, :], 0), axis=1)
        self.facts = jnp.concatenate((active, source, place, swapped))


def quartered(array):
    k, rows, width = array.shape
    return array.reshape(k, 4, rows // 4, width).transpose(1, 0, 2, 3)


def spread(quarters):
    return lax.all_to_all(quarters, "ep", 0, 0, tiled=True, axis_index_groups=planes())


def to_cross(facts, slots, *pools, ahead=0):
    k = pools[0].shape[1]
    rest = pools[0].shape[2:]

    def kernel(facts, *refs):
        for i in range(len(pools)):
            refs[-1][:, i * k : (i + 1) * k] = refs[i][...]

    block = (1, k) + rest
    width = len(pools) * k
    return pl.pallas_call(
        kernel,
        out_shape=jax.ShapeDtypeStruct((slots, width) + rest, pools[0].dtype),
        grid_spec=pltpu.PrefetchScalarGridSpec(
            num_scalar_prefetch=1,
            grid=(slots,),
            in_specs=[pl.BlockSpec(block, lambda i, facts: (facts[ahead + i], 0, 0, 0))] * len(pools),
            out_specs=pl.BlockSpec((1, width) + rest, lambda i, facts: (i, 0, 0, 0)),
        ),
        compiler_params=pltpu.CompilerParams(vmem_limit_bytes=32 * 1024 * 1024),
        cost_estimate=pl.CostEstimate(
            flops=0, transcendentals=0, bytes_accessed=4 * slots * width * pools[0][0, 0].size
        ),
    )(facts, *pools)


def pick(facts, pool, came, *picked):
    slots, k = came.shape[:2]
    rest = came.shape[2:]
    ahead = len(picked) * k

    def kernel(facts, pool, came, *refs):
        out = refs[-1]
        swapped = facts[12 + pl.program_id(0)] == 1

        @pl.when(swapped)
        def _():
            out[:, ahead:] = came[...]

        @pl.when(jnp.logical_not(swapped))
        def _():
            out[:, ahead:] = pool[...]

        for i in range(len(picked)):
            out[:, i * k : (i + 1) * k] = refs[i][...]

    block = (1, k) + rest
    width = ahead + k
    return pl.pallas_call(
        kernel,
        out_shape=jax.ShapeDtypeStruct((4, width) + rest, came.dtype),
        grid_spec=pltpu.PrefetchScalarGridSpec(
            num_scalar_prefetch=1,
            grid=(4,),
            in_specs=[
                pl.BlockSpec(block, lambda i, facts: (facts[4 + i], 0, 0, 0)),
                pl.BlockSpec(block, lambda i, facts: (jnp.minimum(facts[8 + i], slots - 1), 0, 0, 0)),
            ]
            + [pl.BlockSpec(block, lambda i, facts: (i, 0, 0, 0))] * len(picked),
            out_specs=pl.BlockSpec((1, width) + rest, lambda i, facts: (i, 0, 0, 0)),
        ),
        compiler_params=pltpu.CompilerParams(vmem_limit_bytes=32 * 1024 * 1024),
        cost_estimate=pl.CostEstimate(
            flops=0, transcendentals=0, bytes_accessed=2 * (2 * width + k) * pool[:, 0].size
        ),
    )(facts, pool, came, *picked)


def assemble_rows(tok_rows, blocks):
    n, rows, shard = blocks[0].shape
    parts = ((0, tok_rows), (tok_rows, tok_rows), (2 * tok_rows, rows - 2 * tok_rows))

    def kernel(*refs):
        sources, outs, sems = refs[: len(blocks)], refs[len(blocks) : -1], refs[-1]
        copies = [
            pltpu.make_async_copy(
                source.at[:, pl.ds(start, size)], out.at[pl.ds(i * n, n)], sems.at[i, p]
            )
            for i, source in enumerate(sources)
            for p, ((start, size), out) in enumerate(zip(parts, outs))
        ]
        for copy in copies:
            copy.start()
        for copy in copies:
            copy.wait()

    return pl.pallas_call(
        kernel,
        out_shape=tuple(
            jax.ShapeDtypeStruct((len(blocks) * n, size, shard), blocks[0].dtype) for _, size in parts
        ),
        in_specs=[pl.BlockSpec(memory_space=pl.ANY)] * len(blocks),
        out_specs=(pl.BlockSpec(memory_space=pltpu.VMEM),) * 3,
        scratch_shapes=[pltpu.SemaphoreType.DMA((len(blocks), 3))],
        compiler_params=pltpu.CompilerParams(vmem_limit_bytes=32 * 1024 * 1024),
        cost_estimate=pl.CostEstimate(
            flops=0, transcendentals=0, bytes_accessed=4 * len(blocks) * blocks[0].size
        ),
    )(*blocks)


def partial_kernel(x_rows, dy_rows, weight, out):
    for k, rows in enumerate((x_rows, x_rows, dy_rows)):
        out[k] = jnp.dot(rows[...], weight[k], preferred_element_type=jnp.float32).astype(
            jnp.bfloat16
        )


def partial_products(x_rows, dy_rows, weight):
    rows, shard = x_rows.shape
    width = weight.shape[-1]
    size = 256
    return pl.pallas_call(
        partial_kernel,
        out_shape=jax.ShapeDtypeStruct((3, rows, width), jnp.bfloat16),
        grid=(rows // size,),
        in_specs=[
            pl.BlockSpec((size, shard), lambda i: (i, 0)),
            pl.BlockSpec((size, shard), lambda i: (i, 0)),
            pl.BlockSpec((3, shard, width), lambda i: (0, 0, 0)),
        ],
        out_specs=pl.BlockSpec((3, size, width), lambda i: (0, i, 0)),
        compiler_params=pltpu.CompilerParams(vmem_limit_bytes=32 * 1024 * 1024),
        cost_estimate=pl.CostEstimate(
            flops=6 * rows * shard * width,
            transcendentals=0,
            bytes_accessed=2 * (2 * rows * shard + 3 * shard * width + 3 * rows * width),
        ),
    )(x_rows, dy_rows, weight)


def middle_kernel(*refs):
    *addends, scale, down, hidden_ref, d_gate_ref, d_up_ref, left, right = refs

    def total(k):
        value = addends[0][k].astype(jnp.float32)
        for addend in addends[1:]:
            value = value + addend[k].astype(jnp.float32)
        return value

    gate, up, back = total(0), total(1), total(2)
    sigma = jax.nn.sigmoid(gate)
    active = gate * sigma
    hidden = (active * up).astype(jnp.bfloat16)
    hidden_ref[...] = hidden
    d_gate_ref[...] = (back * up * sigma * (1.0 + gate * (1.0 - sigma))).astype(jnp.bfloat16)
    d_up_ref[...] = (back * active).astype(jnp.bfloat16)
    half = left.shape[1]
    for part, out in enumerate((left, right)):
        rows_out = lax.dot_general(
            hidden,
            down[0, part * half : (part + 1) * half],
            (((1,), (1,)), ((), ())),
            preferred_element_type=jnp.float32,
        )
        out[...] = (scale[...] * rows_out).astype(jnp.bfloat16)


def middle(addends, scale, weight):
    _, rows, width = addends[0].shape
    shard = weight.shape[1]
    size = 256
    narrow = jax.ShapeDtypeStruct((rows, width), jnp.bfloat16)
    wide = jax.ShapeDtypeStruct((rows, shard // 2), jnp.bfloat16)
    return pl.pallas_call(
        middle_kernel,
        out_shape=(narrow,) * 3 + (wide,) * 2,
        grid=(rows // size,),
        in_specs=[pl.BlockSpec((3, size, width), lambda i: (0, i, 0))] * len(addends)
        + [
            pl.BlockSpec((size, 1), lambda i: (i, 0)),
            pl.BlockSpec((1, shard, width), lambda i: (2, 0, 0)),
        ],
        out_specs=(pl.BlockSpec((size, width), lambda i: (i, 0)),) * 3
        + (pl.BlockSpec((size, shard // 2), lambda i: (i, 0)),) * 2,
        compiler_params=pltpu.CompilerParams(vmem_limit_bytes=32 * 1024 * 1024),
        cost_estimate=pl.CostEstimate(
            flops=2 * rows * shard * width,
            transcendentals=rows * width,
            bytes_accessed=2 * (9 * rows * width + rows * shard + shard * width),
        ),
    )(*addends, scale, weight)


def collect(quarters):
    quarters = lax.all_to_all(quarters, "ep", 0, 0, tiled=True, axis_index_groups=planes())
    quarters = quarters.transpose(1, 0, 2, 3)
    return quarters.reshape(quarters.shape[0], -1, quarters.shape[-1])


def scatter_plane(left, right):
    size, half = left.shape[0] // 4, left.shape[1]
    left_in = from_partner(left[size : 3 * size], 1)
    right_in = from_partner(right[2 * size :], 2)
    left_last = from_partner(add_rounded(left[3 * size :], left_in[size:]), 2)
    right_last = from_partner(add_rounded(right[size : 2 * size], right_in[:size]), 1)
    left = add_rounded(left[:size], left_in[:size], left_last)
    right = add_rounded(right[:size], right_in[size:], right_last)
    return jnp.concatenate((left, right), axis=1)


def scatter_rest(block):
    for bit in reversed(high_bits(lax.axis_size("ep"))):
        keep = block.shape[0] // 2
        block = add_rounded(block[:keep], from_partner(block[keep:], bit))
    return block


def dot(a, b, dims):
    return lax.dot_general(a, b, ((dims[:1], dims[1:]), ((), ())), preferred_element_type=jnp.float32)


def on_device(
    tokens,
    cotangent,
    expert_ids,
    route_weight,
    placement,
    swap_flags,
    params,
    first_moment,
    second_moment,
):
    experts = lax.axis_size("ep")
    mine = lax.axis_index("ep")
    index = jnp.arange(experts, dtype=jnp.int32)
    table = jnp.sum(
        jnp.where(
            expert_ids.T[None, :, :] == index[:, None, None], route_weight.T[None, :, :], 0.0
        ),
        axis=1,
    )
    tok_rows, shard = tokens.shape
    half = shard // 2
    far = experts // 2

    most = jnp.max(jnp.sum(swap_flags[0].reshape(-1, 4), axis=1))

    def group(part, *operands):
        if lax.axis_size("os") != 2:
            return part(*operands)
        shapes = jax.eval_shape(part, *operands)
        return lax.cond(
            most >= 0,
            part,
            lambda *_: jax.tree.map(lambda x: jnp.zeros(x.shape, x.dtype), shapes),
            *operands,
        )

    terms = []
    for _ in range(3):
        terms.append(lax.reduce_precision(table, 8, 7))
        table = table - terms[-1]
    terms = jnp.stack(terms).astype(jnp.bfloat16).reshape(-1, shard)
    used = terms.shape[0]
    terms = jnp.pad(terms, ((0, -used % 16), (0, 0)))
    block = jnp.concatenate((tokens, cotangent, terms))[None]

    bits = high_bits(experts)

    def over_z(block, params):
        parts = [block]
        for bit in bits[:-1]:
            parts = parts + [from_partner(part, bit) for part in parts]
        other = jnp.concatenate([from_partner(part, bits[-1]) for part in parts])
        block = jnp.concatenate(parts)
        one, two = from_partner(block, 1), from_partner(block, 2)
        pool = spread(quartered(params))
        facts = Migration(swap_flags).facts
        place = placement
        for rnd, bit in enumerate((experts // 2, 1)):
            place = jnp.where(swap_flags[rnd] == 1, place[index ^ bit], place)
        facts = jnp.concatenate((facts, place[mine][None]))
        going = (to_cross(facts, 3, pool), to_cross(facts, 1, pool, ahead=3))
        return block, other, one, two, pool, going, facts

    block, other, one, two, w_pool, w_going, facts = group(over_z, block, params[0])

    def rest(slots, block, other, one, two, w_pool, w_going, facts, first_moment, second_moment):
        return after_z(
            slots, group, tok_rows, used, block, other, one, two, w_pool, w_going, facts,
            first_moment, second_moment,
        )

    operands = (
        block, other, one, two, w_pool, w_going, facts, first_moment[0], second_moment[0],
    )
    if lax.axis_size("os") != 2:
        return rest(4, *operands)
    return lax.cond(
        most <= 3, functools.partial(rest, 3), functools.partial(rest, 4), *operands
    )


def after_z(
    slots, group, tok_rows, used, block, other, one, two, w_pool, w_going, facts,
    first_moment, second_moment,
):
    experts = lax.axis_size("ep")
    far = experts // 2
    shard = block.shape[-1]
    half = shard // 2
    w_came = from_partner(w_going[0] if slots == 3 else jnp.concatenate(w_going), far)

    def to_neighbours(other, one, two, first_moment):
        three = from_partner(two, 1)
        other_one, other_two = from_partner(other, 1), from_partner(other, 2)
        other_three = from_partner(other_one, 2)
        pool = spread(quartered(first_moment))
        return three, other_one, other_two, other_three, pool, to_cross(facts, slots, pool)

    three, other_one, other_two, other_three, m_pool, m_going = group(
        to_neighbours, other, one, two, first_moment
    )
    w_came, m_going = both(w_came, m_going)
    m_came = from_partner(m_going, far)

    def assemble(w_pool, w_came, second_moment, *blocks):
        x_rows, dy_rows, terms = assemble_rows(tok_rows, blocks)
        weight = collect(pick(facts, w_pool, w_came))
        terms = terms[:, :used].reshape(-1, 3, experts, tok_rows)
        terms = lax.dynamic_index_in_dim(terms, facts[16], axis=2, keepdims=False)
        scale = jnp.sum(terms.astype(jnp.float32), axis=1).reshape(-1, 1)
        dy_rows = dy_rows.reshape(-1, shard).astype(jnp.float32)
        dy_rows = (scale * dy_rows).astype(jnp.bfloat16)
        return weight, x_rows.reshape(-1, shard), dy_rows, scale, quartered(second_moment)

    weight, x_rows, dy_rows, scale, v_quarters = group(
        assemble, w_pool, w_came, second_moment,
        block, other, one, other_one, three, other_three, two, other_two,
    )
    def forward(weight, x_rows, dy_rows, scale, v_quarters):
        pool = spread(v_quarters)
        addends = group(over_cores, partial_products(x_rows, dy_rows, weight))
        hidden, d_gate, d_up, *mixed_rows = middle(addends, scale, weight)
        return hidden, d_gate, d_up, mixed_rows, pool

    hidden, d_gate, d_up, mixed_rows, v_pool = group(
        forward, weight, x_rows, dy_rows, scale, v_quarters
    )
    v_going = group(lambda pool: to_cross(facts, slots, pool), v_pool)
    m_came, v_going = both(m_came, v_going)
    v_came = from_partner(v_going, far)

    def backward(weight, x_rows, dy_rows, hidden, d_gate, d_up, mixed_rows, m_pool, m_came):
        mixed = scatter_plane(*mixed_rows)
        grad_rows = [
            (dot(d_gate, weight[0, part], (1, 1)) + dot(d_up, weight[1, part], (1, 1))).astype(
                jnp.bfloat16
            )
            for part in (slice(0, half), slice(half, shard))
        ]
        input_grad = scatter_plane(*grad_rows)
        grad = (
            dot(x_rows, d_gate, (0, 0)),
            dot(x_rows, d_up, (0, 0)),
            dot(dy_rows, hidden, (0, 0)),
        )
        return mixed, input_grad, grad, pick(facts, m_pool, m_came)

    mixed, input_grad, grad, m_picked = group(
        backward, weight, x_rows, dy_rows, hidden, d_gate, d_up, mixed_rows, m_pool, m_came
    )

    def to_owners(mixed, input_grad, m_picked, v_pool, v_came):
        moments = lax.all_to_all(
            pick(facts, v_pool, v_came, m_picked),
            "ep",
            0,
            0,
            tiled=True,
            axis_index_groups=planes(),
        )
        return scatter_rest(mixed), scatter_rest(input_grad), moments

    mixed, input_grad, moments = group(
        to_owners, mixed, input_grad, m_picked, v_pool, v_came
    )
    return (mixed, input_grad, *adam_update(weight, moments, grad))


def solution(mesh):
    state = P("ep", None, "os", None)
    rows = P("ep", "os")
    return jax.shard_map(
        on_device,
        mesh=mesh,
        in_specs=(rows, rows, P("ep", None), P("ep", None), P(), P(), state, state, state),
        out_specs=(rows, rows, state, state, state),
        check_vma=False,
    )
```

```python
import jax
import jax.numpy as jnp
from jax import lax
from jax.experimental import pallas as pl
from jax.experimental.pallas import tpu as pltpu
from jax.sharding import PartitionSpec as P

beta_first = 0.9
beta_second = 0.999
learn_rate = 0.01
adam_eps = 1e-08
adam_count = 10.0


def both(first, second):
    return lax.optimization_barrier((first, second))


def permute(value, pairs):
    return lax.ppermute(value, "ep", pairs)


def from_partner(value, bit):
    return permute(value, [(i, i ^ bit) for i in range(lax.axis_size("ep"))])


def over_cores(value):
    if lax.axis_size("os") != 2:
        return (lax.psum(value, "os"),)
    return value, lax.ppermute(value, "os", [(0, 1), (1, 0)])


def adam_kernel(weight, moments, grad_gate, grad_up, grad_down, new_weight, new_first, new_second):
    for k, grad_ref in enumerate((grad_gate, grad_up, grad_down)):
        grad = grad_ref[...]
        first = beta_first * moments[0, k].astype(jnp.float32) + (1.0 - beta_first) * grad
        second = (
            beta_second * moments[0, 3 + k].astype(jnp.float32) + (1.0 - beta_second) * grad * grad
        )
        step = (learn_rate / (1.0 - beta_first**adam_count)) * first
        size = jnp.sqrt((1.0 / (1.0 - beta_second**adam_count)) * second) + adam_eps
        new_weight[0, k] = (weight[k].astype(jnp.float32) - step / size).astype(jnp.bfloat16)
        new_first[0, k] = first.astype(jnp.bfloat16)
        new_second[0, k] = second.astype(jnp.bfloat16)


def adam_update(weight, moments, grad):
    _, rows, width = weight.shape
    parts = 8 if rows % 128 == 0 else 4
    size = rows // parts
    per_quarter = parts // 4
    state = jax.ShapeDtypeStruct((1, 3, rows, width), jnp.bfloat16)
    return pl.pallas_call(
        adam_kernel,
        out_shape=(state,) * 3,
        grid=(parts,),
        in_specs=[
            pl.BlockSpec((3, size, width), lambda i: (0, i, 0)),
            pl.BlockSpec(
                (1, 6, size, width), lambda i: (i // per_quarter, 0, i % per_quarter, 0)
            ),
        ]
        + [pl.BlockSpec((size, width), lambda i: (i, 0))] * 3,
        out_specs=(pl.BlockSpec((1, 3, size, width), lambda i: (0, 0, i, 0)),) * 3,
        compiler_params=pltpu.CompilerParams(vmem_limit_bytes=32 * 1024 * 1024),
        cost_estimate=pl.CostEstimate(
            flops=40 * weight.size, transcendentals=2 * weight.size, bytes_accessed=16 * weight.size
        ),
    )(weight, moments, *grad)


def high_bits(experts):
    return [1 << b for b in range(experts.bit_length() - 2, 1, -1)]


def add_rounded(*parts):
    total = parts[0].astype(jnp.float32)
    for part in parts[1:]:
        total = total + part.astype(jnp.float32)
    return total.astype(jnp.bfloat16)


def planes():
    return [[i, i + 1, i + 2, i + 3] for i in range(0, lax.axis_size("ep"), 4)]


class Migration:
    def __init__(self, flags):
        mine = lax.axis_index("ep")
        self.mate = mate = mine & 3
        near = lax.dynamic_slice_in_dim(flags, mine - mate, 4, axis=1)
        index = jnp.arange(4, dtype=jnp.int32)
        swaps, turns = near[0], near[1]
        rank = jnp.sum(jnp.where(index[None, :] < index[:, None], swaps[None, :], 0), axis=1)
        chosen = (rank[None, :] == index[:, None]) & (swaps[None, :] == 1)
        active = jnp.sum(jnp.where(chosen, index[None, :], 0), axis=1)
        source = index ^ turns
        at_source = source[:, None] == index[None, :]
        swapped = jnp.sum(jnp.where(at_source, swaps[None, :], 0), axis=1)
        place = jnp.sum(jnp.where(at_source, rank[None, :], 0), axis=1)
        self.facts = jnp.concatenate((active, source, place, swapped))


def quartered(array):
    k, rows, width = array.shape
    return array.reshape(k, 4, rows // 4, width).transpose(1, 0, 2, 3)


def spread(quarters):
    return lax.all_to_all(quarters, "ep", 0, 0, tiled=True, axis_index_groups=planes())


def to_cross(facts, pool):
    block = (1,) + pool.shape[1:]

    def kernel(facts, pool, three, fourth):
        slot = pl.program_id(0)

        @pl.when(slot < 3)
        def _():
            three[...] = pool[...]

        @pl.when(slot == 3)
        def _():
            fourth[...] = pool[...]

    return pl.pallas_call(
        kernel,
        out_shape=tuple(
            jax.ShapeDtypeStruct((slots,) + pool.shape[1:], pool.dtype) for slots in (3, 1)
        ),
        grid_spec=pltpu.PrefetchScalarGridSpec(
            num_scalar_prefetch=1,
            grid=(4,),
            in_specs=[pl.BlockSpec(block, lambda i, facts: (facts[i], 0, 0, 0))],
            out_specs=(
                pl.BlockSpec(block, lambda i, facts: (jnp.minimum(i, 2), 0, 0, 0)),
                pl.BlockSpec(block, lambda i, facts: (0, 0, 0, 0)),
            ),
        ),
        compiler_params=pltpu.CompilerParams(vmem_limit_bytes=32 * 1024 * 1024),
        cost_estimate=pl.CostEstimate(flops=0, transcendentals=0, bytes_accessed=4 * pool.size),
    )(facts, pool)


def across(going):
    return from_partner(going, lax.axis_size("ep") // 2)


def fourth_across(full, going):
    return lax.cond(full, across, lambda going: going, going)


def pick(facts, pool, came, fourth, *picked):
    k = came.shape[1]
    rest = came.shape[2:]
    ahead = len(picked) * k

    def kernel(facts, pool, came, fourth, *refs):
        out = refs[-1]
        dest = pl.program_id(0)
        swapped = facts[12 + dest] == 1
        last = facts[8 + dest] == 3

        @pl.when(swapped & jnp.logical_not(last))
        def _():
            out[:, ahead:] = came[...]

        @pl.when(swapped & last)
        def _():
            out[:, ahead:] = fourth[...]

        @pl.when(jnp.logical_not(swapped))
        def _():
            out[:, ahead:] = pool[...]

        for i in range(len(picked)):
            out[:, i * k : (i + 1) * k] = refs[i][...]

    block = (1, k) + rest
    width = ahead + k
    return pl.pallas_call(
        kernel,
        out_shape=jax.ShapeDtypeStruct((4, width) + rest, came.dtype),
        grid_spec=pltpu.PrefetchScalarGridSpec(
            num_scalar_prefetch=1,
            grid=(4,),
            in_specs=[
                pl.BlockSpec(block, lambda i, facts: (facts[4 + i], 0, 0, 0)),
                pl.BlockSpec(block, lambda i, facts: (jnp.minimum(facts[8 + i], 2), 0, 0, 0)),
                pl.BlockSpec(block, lambda i, facts: (0, 0, 0, 0)),
            ]
            + [pl.BlockSpec(block, lambda i, facts: (i, 0, 0, 0))] * len(picked),
            out_specs=pl.BlockSpec((1, width) + rest, lambda i, facts: (i, 0, 0, 0)),
        ),
        compiler_params=pltpu.CompilerParams(vmem_limit_bytes=32 * 1024 * 1024),
        cost_estimate=pl.CostEstimate(
            flops=0, transcendentals=0, bytes_accessed=2 * (2 * width + k) * pool[:, 0].size
        ),
    )(facts, pool, came, fourth, *picked)


def assemble_rows(tok_rows, blocks):
    n, rows, shard = blocks[0].shape
    parts = ((0, tok_rows), (tok_rows, tok_rows), (2 * tok_rows, rows - 2 * tok_rows))

    def kernel(*refs):
        sources, outs, sems = refs[: len(blocks)], refs[len(blocks) : -1], refs[-1]
        copies = [
            pltpu.make_async_copy(
                source.at[:, pl.ds(start, size)], out.at[pl.ds(i * n, n)], sems.at[i, p]
            )
            for i, source in enumerate(sources)
            for p, ((start, size), out) in enumerate(zip(parts, outs))
        ]
        for copy in copies:
            copy.start()
        for copy in copies:
            copy.wait()

    return pl.pallas_call(
        kernel,
        out_shape=tuple(
            jax.ShapeDtypeStruct((len(blocks) * n, size, shard), blocks[0].dtype) for _, size in parts
        ),
        in_specs=[pl.BlockSpec(memory_space=pl.ANY)] * len(blocks),
        out_specs=(pl.BlockSpec(memory_space=pltpu.VMEM),) * 3,
        scratch_shapes=[pltpu.SemaphoreType.DMA((len(blocks), 3))],
        compiler_params=pltpu.CompilerParams(vmem_limit_bytes=32 * 1024 * 1024),
        cost_estimate=pl.CostEstimate(
            flops=0, transcendentals=0, bytes_accessed=4 * len(blocks) * blocks[0].size
        ),
    )(*blocks)


def partial_kernel(x_rows, dy_rows, weight, out):
    for k, rows in enumerate((x_rows, x_rows, dy_rows)):
        out[k] = jnp.dot(rows[...], weight[k], preferred_element_type=jnp.float32).astype(
            jnp.bfloat16
        )


def partial_products(x_rows, dy_rows, weight):
    rows, shard = x_rows.shape
    width = weight.shape[-1]
    size = 256
    return pl.pallas_call(
        partial_kernel,
        out_shape=jax.ShapeDtypeStruct((3, rows, width), jnp.bfloat16),
        grid=(rows // size,),
        in_specs=[
            pl.BlockSpec((size, shard), lambda i: (i, 0)),
            pl.BlockSpec((size, shard), lambda i: (i, 0)),
            pl.BlockSpec((3, shard, width), lambda i: (0, 0, 0)),
        ],
        out_specs=pl.BlockSpec((3, size, width), lambda i: (0, i, 0)),
        compiler_params=pltpu.CompilerParams(vmem_limit_bytes=32 * 1024 * 1024),
        cost_estimate=pl.CostEstimate(
            flops=6 * rows * shard * width,
            transcendentals=0,
            bytes_accessed=2 * (2 * rows * shard + 3 * shard * width + 3 * rows * width),
        ),
    )(x_rows, dy_rows, weight)


def middle_kernel(*refs):
    *addends, scale, down, hidden_ref, d_gate_ref, d_up_ref, left, right = refs

    def total(k):
        value = addends[0][k].astype(jnp.float32)
        for addend in addends[1:]:
            value = value + addend[k].astype(jnp.float32)
        return value

    gate, up, back = total(0), total(1), total(2)
    sigma = jax.nn.sigmoid(gate)
    active = gate * sigma
    hidden = (active * up).astype(jnp.bfloat16)
    hidden_ref[...] = hidden
    d_gate_ref[...] = (back * up * sigma * (1.0 + gate * (1.0 - sigma))).astype(jnp.bfloat16)
    d_up_ref[...] = (back * active).astype(jnp.bfloat16)
    half = left.shape[1]
    for part, out in enumerate((left, right)):
        rows_out = lax.dot_general(
            hidden,
            down[0, part * half : (part + 1) * half],
            (((1,), (1,)), ((), ())),
            preferred_element_type=jnp.float32,
        )
        out[...] = (scale[...] * rows_out).astype(jnp.bfloat16)


def middle(addends, scale, weight):
    _, rows, width = addends[0].shape
    shard = weight.shape[1]
    size = 256
    narrow = jax.ShapeDtypeStruct((rows, width), jnp.bfloat16)
    wide = jax.ShapeDtypeStruct((rows, shard // 2), jnp.bfloat16)
    return pl.pallas_call(
        middle_kernel,
        out_shape=(narrow,) * 3 + (wide,) * 2,
        grid=(rows // size,),
        in_specs=[pl.BlockSpec((3, size, width), lambda i: (0, i, 0))] * len(addends)
        + [
            pl.BlockSpec((size, 1), lambda i: (i, 0)),
            pl.BlockSpec((1, shard, width), lambda i: (2, 0, 0)),
        ],
        out_specs=(pl.BlockSpec((size, width), lambda i: (i, 0)),) * 3
        + (pl.BlockSpec((size, shard // 2), lambda i: (i, 0)),) * 2,
        compiler_params=pltpu.CompilerParams(vmem_limit_bytes=32 * 1024 * 1024),
        cost_estimate=pl.CostEstimate(
            flops=2 * rows * shard * width,
            transcendentals=rows * width,
            bytes_accessed=2 * (9 * rows * width + rows * shard + shard * width),
        ),
    )(*addends, scale, weight)


def collect(quarters):
    quarters = lax.all_to_all(quarters, "ep", 0, 0, tiled=True, axis_index_groups=planes())
    quarters = quarters.transpose(1, 0, 2, 3)
    return quarters.reshape(quarters.shape[0], -1, quarters.shape[-1])


def scatter_plane(left, right, ahead=()):
    size, half = left.shape[0] // 4, left.shape[1]
    left_out, right_out = left[size : 3 * size], right[2 * size :]
    if ahead:
        left_out, right_out, *ahead = lax.optimization_barrier((left_out, right_out, *ahead))
    return left, right, from_partner(left_out, 1), from_partner(right_out, 2), ahead


def scatter_plane_end(left, right, left_in, right_in):
    size = left.shape[0] // 4
    left_last = from_partner(add_rounded(left[3 * size :], left_in[size:]), 2)
    right_last = from_partner(add_rounded(right[size : 2 * size], right_in[:size]), 1)
    left = add_rounded(left[:size], left_in[:size], left_last)
    right = add_rounded(right[:size], right_in[size:], right_last)
    return jnp.concatenate((left, right), axis=1)


def scatter_rest(block):
    for bit in reversed(high_bits(lax.axis_size("ep"))):
        keep = block.shape[0] // 2
        block = add_rounded(block[:keep], from_partner(block[keep:], bit))
    return block


def dot(a, b, dims):
    return lax.dot_general(a, b, ((dims[:1], dims[1:]), ((), ())), preferred_element_type=jnp.float32)


def on_device(
    tokens,
    cotangent,
    expert_ids,
    route_weight,
    placement,
    swap_flags,
    params,
    first_moment,
    second_moment,
):
    experts = lax.axis_size("ep")
    mine = lax.axis_index("ep")
    index = jnp.arange(experts, dtype=jnp.int32)
    table = jnp.sum(
        jnp.where(
            expert_ids.T[None, :, :] == index[:, None, None], route_weight.T[None, :, :], 0.0
        ),
        axis=1,
    )
    tok_rows, shard = tokens.shape
    half = shard // 2
    far = experts // 2

    def group(part, *operands):
        if lax.axis_size("os") != 2:
            return part(*operands)
        shapes = jax.eval_shape(part, *operands)
        return lax.cond(
            swap_flags[0, 0] >= 0,
            part,
            lambda *_: jax.tree.map(lambda x: jnp.zeros(x.shape, x.dtype), shapes),
            *operands,
        )

    terms = []
    for _ in range(3):
        terms.append(lax.reduce_precision(table, 8, 7))
        table = table - terms[-1]
    terms = jnp.stack(terms).astype(jnp.bfloat16).reshape(-1, shard)
    used = terms.shape[0]
    terms = jnp.pad(terms, ((0, -used % 16), (0, 0)))
    block = jnp.concatenate((tokens, cotangent, terms))[None]

    bits = high_bits(experts)

    def over_z(block, params):
        parts = [block]
        for bit in bits[:-1]:
            parts = parts + [from_partner(part, bit) for part in parts]
        other = jnp.concatenate([from_partner(part, bits[-1]) for part in parts])
        block = jnp.concatenate(parts)
        one, two = from_partner(block, 1), from_partner(block, 2)
        pool = spread(quartered(params))
        facts = Migration(swap_flags).facts
        place = placement
        for rnd, bit in enumerate((experts // 2, 1)):
            place = jnp.where(swap_flags[rnd] == 1, place[index ^ bit], place)
        facts = jnp.concatenate((facts, place[mine][None]))
        full = jnp.any(jnp.sum(swap_flags[0].reshape(-1, 4), axis=1) > 3)
        return block, other, one, two, pool, to_cross(facts, pool), facts, full

    block, other, one, two, w_pool, w_going, facts, full = group(over_z, block, params[0])

    w_three, w_fourth = w_going
    w_came = across(w_three)

    def to_neighbours(other, one, two, first_moment):
        three = from_partner(two, 1)
        other_one, other_two = from_partner(other, 1), from_partner(other, 2)
        other_three = from_partner(other_one, 2)
        pool = spread(quartered(first_moment))
        return three, other_one, other_two, other_three, pool, to_cross(facts, pool)

    three, other_one, other_two, other_three, m_pool, (m_three, m_fourth) = group(
        to_neighbours, other, one, two, first_moment[0]
    )
    w_came, w_fourth = both(w_came, w_fourth)
    w_fourth = fourth_across(full, w_fourth)
    w_fourth, m_three = both(w_fourth, m_three)
    m_came = across(m_three)

    def assemble(w_pool, w_came, w_fourth, second_moment, *blocks):
        x_rows, dy_rows, terms = assemble_rows(tok_rows, blocks)
        weight = collect(pick(facts, w_pool, w_came, w_fourth))
        terms = terms[:, :used].reshape(-1, 3, experts, tok_rows)
        terms = lax.dynamic_index_in_dim(terms, facts[16], axis=2, keepdims=False)
        scale = jnp.sum(terms.astype(jnp.float32), axis=1).reshape(-1, 1)
        dy_rows = dy_rows.reshape(-1, shard).astype(jnp.float32)
        dy_rows = (scale * dy_rows).astype(jnp.bfloat16)
        return weight, x_rows.reshape(-1, shard), dy_rows, scale, quartered(second_moment)

    weight, x_rows, dy_rows, scale, v_quarters = group(
        assemble, w_pool, w_came, w_fourth, second_moment[0],
        block, other, one, other_one, three, other_three, two, other_two,
    )
    def forward(weight, x_rows, dy_rows, scale, v_quarters):
        pool = spread(v_quarters)
        addends = group(over_cores, partial_products(x_rows, dy_rows, weight))
        hidden, d_gate, d_up, *mixed_rows = middle(addends, scale, weight)
        return hidden, d_gate, d_up, mixed_rows, pool

    hidden, d_gate, d_up, mixed_rows, v_pool = group(
        forward, weight, x_rows, dy_rows, scale, v_quarters
    )
    v_three, v_fourth = group(lambda pool: to_cross(facts, pool), v_pool)
    m_came, m_fourth = both(m_came, m_fourth)
    m_fourth = fourth_across(full, m_fourth)
    m_fourth, v_three = both(m_fourth, v_three)
    v_came = across(v_three)

    def backward(weight, x_rows, dy_rows, hidden, d_gate, d_up, mixed_rows, m_pool, m_came, m_fourth):
        left, right, left_in, right_in, _ = scatter_plane(*mixed_rows)
        grad_rows = [
            (dot(d_gate, weight[0, part], (1, 1)) + dot(d_up, weight[1, part], (1, 1))).astype(
                jnp.bfloat16
            )
            for part in (slice(0, half), slice(half, shard))
        ]
        *gone, (left_in, right_in) = scatter_plane(*grad_rows, ahead=(left_in, right_in))
        mixed = scatter_plane_end(left, right, left_in, right_in)
        input_grad = scatter_plane_end(*gone)
        grad = (
            dot(x_rows, d_gate, (0, 0)),
            dot(x_rows, d_up, (0, 0)),
            dot(dy_rows, hidden, (0, 0)),
        )
        return mixed, input_grad, grad, pick(facts, m_pool, m_came, m_fourth)

    mixed, input_grad, grad, m_picked = group(
        backward, weight, x_rows, dy_rows, hidden, d_gate, d_up, mixed_rows, m_pool, m_came, m_fourth
    )
    v_came, v_fourth = both(v_came, v_fourth)
    v_fourth = fourth_across(full, v_fourth)

    def to_owners(mixed, input_grad, m_picked, v_pool, v_came, v_fourth):
        moments = lax.all_to_all(
            pick(facts, v_pool, v_came, v_fourth, m_picked),
            "ep",
            0,
            0,
            tiled=True,
            axis_index_groups=planes(),
        )
        return scatter_rest(mixed), scatter_rest(input_grad), moments

    mixed, input_grad, moments = group(
        to_owners, mixed, input_grad, m_picked, v_pool, v_came, v_fourth
    )
    return (mixed, input_grad, *adam_update(weight, moments, grad))


def solution(mesh):
    state = P("ep", None, "os", None)
    rows = P("ep", "os")
    return jax.shard_map(
        on_device,
        mesh=mesh,
        in_specs=(rows, rows, P("ep", None), P("ep", None), P(), P(), state, state, state),
        out_specs=(rows, rows, state, state, state),
        check_vma=False,
    )
```

```python
import jax
import jax.numpy as jnp
from jax import lax
from jax.experimental import pallas as pl
from jax.experimental.pallas import tpu as pltpu
from jax.sharding import PartitionSpec as P

beta_first = 0.9
beta_second = 0.999
learn_rate = 0.01
adam_eps = 1e-08
adam_count = 10.0


def both(first, second):
    return lax.optimization_barrier((first, second))


def permute(value, pairs):
    return lax.ppermute(value, "ep", pairs)


def from_partner(value, bit):
    return permute(value, [(i, i ^ bit) for i in range(lax.axis_size("ep"))])


def over_cores(value):
    if lax.axis_size("os") != 2:
        return (lax.psum(value, "os"),)
    return value, lax.ppermute(value, "os", [(0, 1), (1, 0)])


def adam_kernel(weight, moments, grad_gate, grad_up, grad_down, new_weight, new_first, new_second):
    for k, grad_ref in enumerate((grad_gate, grad_up, grad_down)):
        grad = grad_ref[...]
        first = beta_first * moments[0, k].astype(jnp.float32) + (1.0 - beta_first) * grad
        second = (
            beta_second * moments[0, 3 + k].astype(jnp.float32) + (1.0 - beta_second) * grad * grad
        )
        step = (learn_rate / (1.0 - beta_first**adam_count)) * first
        size = jnp.sqrt((1.0 / (1.0 - beta_second**adam_count)) * second) + adam_eps
        new_weight[0, k] = (weight[k].astype(jnp.float32) - step / size).astype(jnp.bfloat16)
        new_first[0, k] = first.astype(jnp.bfloat16)
        new_second[0, k] = second.astype(jnp.bfloat16)


def adam_update(weight, moments, grad):
    _, rows, width = weight.shape
    parts = 8 if rows % 128 == 0 else 4
    size = rows // parts
    per_quarter = parts // 4
    state = jax.ShapeDtypeStruct((1, 3, rows, width), jnp.bfloat16)
    return pl.pallas_call(
        adam_kernel,
        out_shape=(state,) * 3,
        grid=(parts,),
        in_specs=[
            pl.BlockSpec((3, size, width), lambda i: (0, i, 0)),
            pl.BlockSpec(
                (1, 6, size, width), lambda i: (i // per_quarter, 0, i % per_quarter, 0)
            ),
        ]
        + [pl.BlockSpec((size, width), lambda i: (i, 0))] * 3,
        out_specs=(pl.BlockSpec((1, 3, size, width), lambda i: (0, 0, i, 0)),) * 3,
        compiler_params=pltpu.CompilerParams(vmem_limit_bytes=32 * 1024 * 1024),
        cost_estimate=pl.CostEstimate(
            flops=40 * weight.size, transcendentals=2 * weight.size, bytes_accessed=16 * weight.size
        ),
    )(weight, moments, *grad)


def high_bits(experts):
    return [1 << b for b in range(experts.bit_length() - 2, 1, -1)]


def add_rounded(*parts):
    total = parts[0].astype(jnp.float32)
    for part in parts[1:]:
        total = total + part.astype(jnp.float32)
    return total.astype(jnp.bfloat16)


def planes():
    return [[i, i + 1, i + 2, i + 3] for i in range(0, lax.axis_size("ep"), 4)]


class Migration:
    def __init__(self, flags):
        mine = lax.axis_index("ep")
        self.mate = mate = mine & 3
        near = lax.dynamic_slice_in_dim(flags, mine - mate, 4, axis=1)
        index = jnp.arange(4, dtype=jnp.int32)
        swaps, turns = near[0], near[1]
        rank = jnp.sum(jnp.where(index[None, :] < index[:, None], swaps[None, :], 0), axis=1)
        chosen = (rank[None, :] == index[:, None]) & (swaps[None, :] == 1)
        active = jnp.sum(jnp.where(chosen, index[None, :], 0), axis=1)
        source = index ^ turns
        at_source = source[:, None] == index[None, :]
        swapped = jnp.sum(jnp.where(at_source, swaps[None, :], 0), axis=1)
        place = jnp.sum(jnp.where(at_source, rank[None, :], 0), axis=1)
        self.facts = jnp.concatenate((active, source, place, swapped))


def quartered(array):
    k, rows, width = array.shape
    return array.reshape(k, 4, rows // 4, width).transpose(1, 0, 2, 3)


def spread(quarters):
    return lax.all_to_all(quarters, "ep", 0, 0, tiled=True, axis_index_groups=planes())


def to_cross(facts, pool):
    block = (1,) + pool.shape[1:]

    def kernel(facts, pool, three, fourth):
        slot = pl.program_id(0)

        @pl.when(slot < 3)
        def _():
            three[...] = pool[...]

        @pl.when(slot == 3)
        def _():
            fourth[...] = pool[...]

    return pl.pallas_call(
        kernel,
        out_shape=tuple(
            jax.ShapeDtypeStruct((slots,) + pool.shape[1:], pool.dtype) for slots in (3, 1)
        ),
        grid_spec=pltpu.PrefetchScalarGridSpec(
            num_scalar_prefetch=1,
            grid=(4,),
            in_specs=[pl.BlockSpec(block, lambda i, facts: (facts[i], 0, 0, 0))],
            out_specs=(
                pl.BlockSpec(block, lambda i, facts: (jnp.minimum(i, 2), 0, 0, 0)),
                pl.BlockSpec(block, lambda i, facts: (0, 0, 0, 0)),
            ),
        ),
        compiler_params=pltpu.CompilerParams(vmem_limit_bytes=32 * 1024 * 1024),
        cost_estimate=pl.CostEstimate(flops=0, transcendentals=0, bytes_accessed=4 * pool.size),
    )(facts, pool)


def across(going):
    return from_partner(going, lax.axis_size("ep") // 2)


def fourth_across(full, going):
    experts = lax.axis_size("ep")

    def only(parity):
        return [
            (i, i ^ (experts // 2) if (i >> 2) % 2 == parity else i ^ 1) for i in range(experts)
        ]

    return lax.switch(
        full,
        (
            lambda going: going,
            lambda going: permute(going, only(0)),
            lambda going: permute(going, only(1)),
            across,
        ),
        going,
    )


def pick(facts, pool, came, fourth, *picked):
    k = came.shape[1]
    rest = came.shape[2:]
    ahead = len(picked) * k

    def kernel(facts, pool, came, fourth, *refs):
        out = refs[-1]
        dest = pl.program_id(0)
        swapped = facts[12 + dest] == 1
        last = facts[8 + dest] == 3

        @pl.when(swapped & jnp.logical_not(last))
        def _():
            out[:, ahead:] = came[...]

        @pl.when(swapped & last)
        def _():
            out[:, ahead:] = fourth[...]

        @pl.when(jnp.logical_not(swapped))
        def _():
            out[:, ahead:] = pool[...]

        for i in range(len(picked)):
            out[:, i * k : (i + 1) * k] = refs[i][...]

    block = (1, k) + rest
    width = ahead + k
    return pl.pallas_call(
        kernel,
        out_shape=jax.ShapeDtypeStruct((4, width) + rest, came.dtype),
        grid_spec=pltpu.PrefetchScalarGridSpec(
            num_scalar_prefetch=1,
            grid=(4,),
            in_specs=[
                pl.BlockSpec(block, lambda i, facts: (facts[4 + i], 0, 0, 0)),
                pl.BlockSpec(block, lambda i, facts: (jnp.minimum(facts[8 + i], 2), 0, 0, 0)),
                pl.BlockSpec(block, lambda i, facts: (0, 0, 0, 0)),
            ]
            + [pl.BlockSpec(block, lambda i, facts: (i, 0, 0, 0))] * len(picked),
            out_specs=pl.BlockSpec((1, width) + rest, lambda i, facts: (i, 0, 0, 0)),
        ),
        compiler_params=pltpu.CompilerParams(vmem_limit_bytes=32 * 1024 * 1024),
        cost_estimate=pl.CostEstimate(
            flops=0, transcendentals=0, bytes_accessed=2 * (2 * width + k) * pool[:, 0].size
        ),
    )(facts, pool, came, fourth, *picked)


def assemble_rows(tok_rows, blocks):
    n, rows, shard = blocks[0].shape
    parts = ((0, tok_rows), (tok_rows, tok_rows), (2 * tok_rows, rows - 2 * tok_rows))

    def kernel(*refs):
        sources, outs, sems = refs[: len(blocks)], refs[len(blocks) : -1], refs[-1]
        copies = [
            pltpu.make_async_copy(
                source.at[:, pl.ds(start, size)], out.at[pl.ds(i * n, n)], sems.at[i, p]
            )
            for i, source in enumerate(sources)
            for p, ((start, size), out) in enumerate(zip(parts, outs))
        ]
        for copy in copies:
            copy.start()
        for copy in copies:
            copy.wait()

    return pl.pallas_call(
        kernel,
        out_shape=tuple(
            jax.ShapeDtypeStruct((len(blocks) * n, size, shard), blocks[0].dtype) for _, size in parts
        ),
        in_specs=[pl.BlockSpec(memory_space=pl.ANY)] * len(blocks),
        out_specs=(pl.BlockSpec(memory_space=pltpu.VMEM),) * 3,
        scratch_shapes=[pltpu.SemaphoreType.DMA((len(blocks), 3))],
        compiler_params=pltpu.CompilerParams(vmem_limit_bytes=32 * 1024 * 1024),
        cost_estimate=pl.CostEstimate(
            flops=0, transcendentals=0, bytes_accessed=4 * len(blocks) * blocks[0].size
        ),
    )(*blocks)


def partial_kernel(x_rows, dy_rows, weight, out):
    for k, rows in enumerate((x_rows, x_rows, dy_rows)):
        out[k] = jnp.dot(rows[...], weight[k], preferred_element_type=jnp.float32).astype(
            jnp.bfloat16
        )


def partial_products(x_rows, dy_rows, weight):
    rows, shard = x_rows.shape
    width = weight.shape[-1]
    size = 256
    return pl.pallas_call(
        partial_kernel,
        out_shape=jax.ShapeDtypeStruct((3, rows, width), jnp.bfloat16),
        grid=(rows // size,),
        in_specs=[
            pl.BlockSpec((size, shard), lambda i: (i, 0)),
            pl.BlockSpec((size, shard), lambda i: (i, 0)),
            pl.BlockSpec((3, shard, width), lambda i: (0, 0, 0)),
        ],
        out_specs=pl.BlockSpec((3, size, width), lambda i: (0, i, 0)),
        compiler_params=pltpu.CompilerParams(vmem_limit_bytes=32 * 1024 * 1024),
        cost_estimate=pl.CostEstimate(
            flops=6 * rows * shard * width,
            transcendentals=0,
            bytes_accessed=2 * (2 * rows * shard + 3 * shard * width + 3 * rows * width),
        ),
    )(x_rows, dy_rows, weight)


def middle_kernel(*refs):
    *addends, scale, down, hidden_ref, d_gate_ref, d_up_ref, left, right = refs

    def total(k):
        value = addends[0][k].astype(jnp.float32)
        for addend in addends[1:]:
            value = value + addend[k].astype(jnp.float32)
        return value

    gate, up, back = total(0), total(1), total(2)
    sigma = jax.nn.sigmoid(gate)
    active = gate * sigma
    hidden = (active * up).astype(jnp.bfloat16)
    hidden_ref[...] = hidden
    d_gate_ref[...] = (back * up * sigma * (1.0 + gate * (1.0 - sigma))).astype(jnp.bfloat16)
    d_up_ref[...] = (back * active).astype(jnp.bfloat16)
    half = left.shape[1]
    for part, out in enumerate((left, right)):
        rows_out = lax.dot_general(
            hidden,
            down[0, part * half : (part + 1) * half],
            (((1,), (1,)), ((), ())),
            preferred_element_type=jnp.float32,
        )
        out[...] = (scale[...] * rows_out).astype(jnp.bfloat16)


def middle(addends, scale, weight):
    _, rows, width = addends[0].shape
    shard = weight.shape[1]
    size = 256
    narrow = jax.ShapeDtypeStruct((rows, width), jnp.bfloat16)
    wide = jax.ShapeDtypeStruct((rows, shard // 2), jnp.bfloat16)
    return pl.pallas_call(
        middle_kernel,
        out_shape=(narrow,) * 3 + (wide,) * 2,
        grid=(rows // size,),
        in_specs=[pl.BlockSpec((3, size, width), lambda i: (0, i, 0))] * len(addends)
        + [
            pl.BlockSpec((size, 1), lambda i: (i, 0)),
            pl.BlockSpec((1, shard, width), lambda i: (2, 0, 0)),
        ],
        out_specs=(pl.BlockSpec((size, width), lambda i: (i, 0)),) * 3
        + (pl.BlockSpec((size, shard // 2), lambda i: (i, 0)),) * 2,
        compiler_params=pltpu.CompilerParams(vmem_limit_bytes=32 * 1024 * 1024),
        cost_estimate=pl.CostEstimate(
            flops=2 * rows * shard * width,
            transcendentals=rows * width,
            bytes_accessed=2 * (9 * rows * width + rows * shard + shard * width),
        ),
    )(*addends, scale, weight)


def collect(quarters):
    quarters = lax.all_to_all(quarters, "ep", 0, 0, tiled=True, axis_index_groups=planes())
    quarters = quarters.transpose(1, 0, 2, 3)
    return quarters.reshape(quarters.shape[0], -1, quarters.shape[-1])


def scatter_plane(left, right, ahead=()):
    size, half = left.shape[0] // 4, left.shape[1]
    left_out, right_out = left[size : 3 * size], right[2 * size :]
    if ahead:
        left_out, right_out, *ahead = lax.optimization_barrier((left_out, right_out, *ahead))
    return left, right, from_partner(left_out, 1), from_partner(right_out, 2), ahead


def scatter_plane_end(left, right, left_in, right_in):
    size = left.shape[0] // 4
    left_last = from_partner(add_rounded(left[3 * size :], left_in[size:]), 2)
    right_last = from_partner(add_rounded(right[size : 2 * size], right_in[:size]), 1)
    left = add_rounded(left[:size], left_in[:size], left_last)
    right = add_rounded(right[:size], right_in[size:], right_last)
    return jnp.concatenate((left, right), axis=1)


def scatter_rest(block):
    for bit in reversed(high_bits(lax.axis_size("ep"))):
        keep = block.shape[0] // 2
        block = add_rounded(block[:keep], from_partner(block[keep:], bit))
    return block


def dot(a, b, dims):
    return lax.dot_general(a, b, ((dims[:1], dims[1:]), ((), ())), preferred_element_type=jnp.float32)


def on_device(
    tokens,
    cotangent,
    expert_ids,
    route_weight,
    placement,
    swap_flags,
    params,
    first_moment,
    second_moment,
):
    experts = lax.axis_size("ep")
    mine = lax.axis_index("ep")
    index = jnp.arange(experts, dtype=jnp.int32)
    table = jnp.sum(
        jnp.where(
            expert_ids.T[None, :, :] == index[:, None, None], route_weight.T[None, :, :], 0.0
        ),
        axis=1,
    )
    tok_rows, shard = tokens.shape
    half = shard // 2
    far = experts // 2

    def group(part, *operands):
        if lax.axis_size("os") != 2:
            return part(*operands)
        shapes = jax.eval_shape(part, *operands)
        return lax.cond(
            swap_flags[0, 0] >= 0,
            part,
            lambda *_: jax.tree.map(lambda x: jnp.zeros(x.shape, x.dtype), shapes),
            *operands,
        )

    terms = []
    for _ in range(3):
        terms.append(lax.reduce_precision(table, 8, 7))
        table = table - terms[-1]
    terms = jnp.stack(terms).astype(jnp.bfloat16).reshape(-1, shard)
    used = terms.shape[0]
    terms = jnp.pad(terms, ((0, -used % 16), (0, 0)))
    block = jnp.concatenate((tokens, cotangent, terms))[None]

    bits = high_bits(experts)

    def over_z(block, params):
        parts = [block]
        for bit in bits[:-1]:
            parts = parts + [from_partner(part, bit) for part in parts]
        other = jnp.concatenate([from_partner(part, bits[-1]) for part in parts])
        block = jnp.concatenate(parts)
        one, two = from_partner(block, 1), from_partner(block, 2)
        pool = spread(quartered(params))
        facts = Migration(swap_flags).facts
        place = placement
        for rnd, bit in enumerate((experts // 2, 1)):
            place = jnp.where(swap_flags[rnd] == 1, place[index ^ bit], place)
        facts = jnp.concatenate((facts, place[mine][None]))
        full = jnp.any(jnp.sum(swap_flags[0].reshape(-1, 2, 4), axis=2) > 3, axis=0)
        full = jnp.sum(jnp.where(full, jnp.array([1, 2], jnp.int32), 0))
        return block, other, one, two, pool, to_cross(facts, pool), facts, full

    block, other, one, two, w_pool, w_going, facts, full = group(over_z, block, params[0])

    w_three, w_fourth = w_going
    w_came = across(w_three)

    def to_neighbours(other, one, two, first_moment):
        three = from_partner(two, 1)
        other_one, other_two = from_partner(other, 1), from_partner(other, 2)
        other_three = from_partner(other_one, 2)
        pool = spread(quartered(first_moment))
        return three, other_one, other_two, other_three, pool, to_cross(facts, pool)

    three, other_one, other_two, other_three, m_pool, (m_three, m_fourth) = group(
        to_neighbours, other, one, two, first_moment[0]
    )
    w_came, w_fourth = both(w_came, w_fourth)
    w_fourth = fourth_across(full, w_fourth)
    w_fourth, m_three = both(w_fourth, m_three)
    m_came = across(m_three)

    def assemble(w_pool, w_came, w_fourth, second_moment, *blocks):
        x_rows, dy_rows, terms = assemble_rows(tok_rows, blocks)
        weight = collect(pick(facts, w_pool, w_came, w_fourth))
        terms = terms[:, :used].reshape(-1, 3, experts, tok_rows)
        terms = lax.dynamic_index_in_dim(terms, facts[16], axis=2, keepdims=False)
        scale = jnp.sum(terms.astype(jnp.float32), axis=1).reshape(-1, 1)
        dy_rows = dy_rows.reshape(-1, shard).astype(jnp.float32)
        dy_rows = (scale * dy_rows).astype(jnp.bfloat16)
        return weight, x_rows.reshape(-1, shard), dy_rows, scale, quartered(second_moment)

    weight, x_rows, dy_rows, scale, v_quarters = group(
        assemble, w_pool, w_came, w_fourth, second_moment[0],
        block, other, one, other_one, three, other_three, two, other_two,
    )
    def forward(weight, x_rows, dy_rows, scale, v_quarters):
        pool = spread(v_quarters)
        addends = group(over_cores, partial_products(x_rows, dy_rows, weight))
        hidden, d_gate, d_up, *mixed_rows = middle(addends, scale, weight)
        return hidden, d_gate, d_up, mixed_rows, pool

    hidden, d_gate, d_up, mixed_rows, v_pool = group(
        forward, weight, x_rows, dy_rows, scale, v_quarters
    )
    v_three, v_fourth = group(lambda pool: to_cross(facts, pool), v_pool)
    m_came, m_fourth = both(m_came, m_fourth)
    m_fourth = fourth_across(full, m_fourth)
    m_fourth, v_three = both(m_fourth, v_three)
    v_came = across(v_three)

    def backward(weight, x_rows, dy_rows, hidden, d_gate, d_up, mixed_rows, m_pool, m_came, m_fourth):
        left, right, left_in, right_in, _ = scatter_plane(*mixed_rows)
        grad_rows = [
            (dot(d_gate, weight[0, part], (1, 1)) + dot(d_up, weight[1, part], (1, 1))).astype(
                jnp.bfloat16
            )
            for part in (slice(0, half), slice(half, shard))
        ]
        *gone, (left_in, right_in) = scatter_plane(*grad_rows, ahead=(left_in, right_in))
        mixed = scatter_plane_end(left, right, left_in, right_in)
        input_grad = scatter_plane_end(*gone)
        grad = (
            dot(x_rows, d_gate, (0, 0)),
            dot(x_rows, d_up, (0, 0)),
            dot(dy_rows, hidden, (0, 0)),
        )
        return mixed, input_grad, grad, pick(facts, m_pool, m_came, m_fourth)

    mixed, input_grad, grad, m_picked = group(
        backward, weight, x_rows, dy_rows, hidden, d_gate, d_up, mixed_rows, m_pool, m_came, m_fourth
    )
    v_came, v_fourth = both(v_came, v_fourth)
    v_fourth = fourth_across(full, v_fourth)

    def to_owners(mixed, input_grad, m_picked, v_pool, v_came, v_fourth):
        moments = lax.all_to_all(
            pick(facts, v_pool, v_came, v_fourth, m_picked),
            "ep",
            0,
            0,
            tiled=True,
            axis_index_groups=planes(),
        )
        return scatter_rest(mixed), scatter_rest(input_grad), moments

    mixed, input_grad, moments = group(
        to_owners, mixed, input_grad, m_picked, v_pool, v_came, v_fourth
    )
    return (mixed, input_grad, *adam_update(weight, moments, grad))


def solution(mesh):
    state = P("ep", None, "os", None)
    rows = P("ep", "os")
    return jax.shard_map(
        on_device,
        mesh=mesh,
        in_specs=(rows, rows, P("ep", None), P("ep", None), P(), P(), state, state, state),
        out_specs=(rows, rows, state, state, state),
        check_vma=False,
    )
```
